32 devices in a mesh: gy: 8 (over z, y), gz: 4 (over x, core).
Axes of the slice: x: 2, y: 2, z: 4, core: 2. Of those that a mesh axis runs over, the one named last changes fastest.
Arguments:
- thermal_state: float32 [32, 1024, 512], P(None, 'gy', 'gz'), may hold values from -6 to 6
- fourier_ratio_width: float32 [32], replicated, may hold values from 50 to 5000
- fourier_ratio_height: float32 [32], replicated, may hold values from 50 to 5000
Outputs:
- stepped: float32 [32, 1024, 512], P(None, 'gy', 'gz')
The draws below stay inside these ranges and needn't reach their ends.
All inputs are finite; a program needn't handle non-finite values.
Results may differ from the reference program's by a relative error of at most 0.0005.
Values sent between devices are 32-bit elements; how exact they have to be, the bound alone decides.
No kernel may reach another device: no remote copies, remote signals or barrier semaphores. Data moves between devices by JAX's collectives and lax.ppermute only.
A program may use at most 128 MiB of HBM per device.

```python
import math
import jax
import jax.numpy as jnp
from jax import lax

SHEET_TOTAL = 32
WIDTH_NODES = 1024
HEIGHT_NODES = 512


def level_of(rng, extent, shards, least, top_value):
    gain, own = 1.0, jax.random.fold_in(rng, 6)
    for position, shards_of in shards:
        heights = jnp.exp(jax.random.uniform(jax.random.fold_in(own, position), (shards_of,), jnp.float32, least / len(shards), top_value / len(shards)))
        gain = gain * jnp.repeat(heights, extent[position] // shards_of).reshape([-1 if axis == position else 1 for axis in range(len(extent))])
    return gain


def centred(stream_key, shape, width, bound, split=(), kind=jnp.bfloat16):
    factor_of = level_of(stream_key, shape, split, -0.22, 0.18) if split else 1.0
    array = jax.random.normal(stream_key, shape, jnp.float32) * width * factor_of
    return jnp.minimum(jnp.maximum(array, -bound), bound).astype(kind)


def setup_inputs(seed: int = 0) -> dict:
    key_list = jax.random.split(jax.random.key(seed), 4)
    return {
        "thermal_state": centred(key_list[0], (SHEET_TOTAL, WIDTH_NODES, HEIGHT_NODES), 1.0, 6.0, ((1, 8), (2, 4)), jnp.float32),
        "fourier_ratio_width": jnp.clip(jnp.exp(jax.random.uniform(key_list[1], (SHEET_TOTAL,), jnp.float32, math.log(50.0), math.log(5000.0))), 50.0, 5000.0),
        "fourier_ratio_height": jnp.clip(jnp.exp(jax.random.uniform(key_list[2], (SHEET_TOTAL,), jnp.float32, math.log(50.0), math.log(5000.0))), 50.0, 5000.0),
    }


compact_alpha = 2.0 / 11.0
inner_weight = 12.0 / 11.0
outer_weight = 3.0 / 44.0

def compact_source(extended_temps, diffusion):
    centre = extended_temps[2:-2]
    nearby = extended_temps[1:-3] + extended_temps[3:-1]
    distant = extended_temps[4:] + extended_temps[:-4]
    return compact_alpha * nearby + centre + diffusion * outer_weight * (distant - 2.0 * centre)

def solve_lines(diffusion, source):
    length = source.shape[0]
    beside = compact_alpha - inner_weight * diffusion
    centre = 1.0 + 2.0 * inner_weight * diffusion
    indices = jnp.arange(length)
    sub_diag = jnp.where(indices > 0, beside, 0.0 * beside)
    super_diag = jnp.where(indices < length - 1, beside, 0.0 * beside)
    main_diag = jnp.zeros((length,), source.dtype) + centre
    return lax.linalg.tridiagonal_solve(sub_diag[None], main_diag[None], super_diag[None], source[None])[0]

def lone_sheet(plane_items):
    plane_field, rate_along_y, rate_along_z = plane_items
    extended_temps = jnp.pad(plane_field, ((2, 2), (0, 0)))
    halfway = solve_lines(rate_along_y, compact_source(extended_temps, rate_along_y))
    turned = jnp.pad(halfway.T, ((2, 2), (0, 0)))
    return solve_lines(rate_along_z, compact_source(turned, rate_along_z)).T

def reference(thermal_state, fourier_ratio_width, fourier_ratio_height):
    return lax.map(lone_sheet, (thermal_state, fourier_ratio_width, fourier_ratio_height))
```

```python
import functools

import jax
import jax.numpy as jnp
from jax import lax
from jax.experimental import pallas as pl
from jax.experimental.pallas import tpu as pltpu
from jax.sharding import PartitionSpec as P

alpha = 2.0 / 11.0
inner_weight = 12.0 / 11.0
outer_weight = 3.0 / 44.0
F32 = jnp.float32
BF16 = jnp.bfloat16
STEPS = 4
VMEM = 24 * 1024 * 1024


def spread(rates, table):
    for k in range(table.shape[0]):
        table[pl.ds(k, 1), :] = jnp.full((1, table.shape[1]), rates[k], F32)


class Line:
    def __init__(self, rate, position, devices, m):
        beside = inner_weight * rate - alpha
        eps = (1.0 + 2.0 * alpha) / (2.0 * beside)
        sinh = jnp.sqrt(eps * (2.0 + eps))
        corner = rate * outer_weight
        self.m = m
        self.theta = jnp.log1p(eps + sinh)
        total = m * devices
        self.far = total + 1 - m * position
        self.near = m * position
        self.c = m // 2
        self.green = 1.0 / (2.0 * beside * sinh * (1.0 - self.power(2 * (total + 1))))
        self.rho = 1.0 + 2.0 * alpha * (1.0 + eps) + 4.0 * corner * eps * (2.0 + eps)
        self.side = -corner / beside
        self.mid = 2.0 * self.side * (1.0 + eps) - alpha / beside
        self.corner = corner
        self.is_first = jnp.where(position == 0, 1.0, 0.0).astype(F32)
        self.is_last = jnp.where(position == devices - 1, 1.0, 0.0).astype(F32)
        self.cell = lax.broadcasted_iota(jnp.int32, rate.shape, 1)

    def power(self, n):
        return jnp.exp(-self.theta * jnp.asarray(n, F32))

    def vectors(self):
        i = (self.cell + (1 - self.c)).astype(F32)
        down, up = jnp.exp(-self.theta * i), jnp.exp(self.theta * i)
        self.cut_far = self.power(2 * (self.far - self.c))
        self.cut_near = self.power(2 * (self.near + self.c))
        self.phi = down - self.cut_far * up
        self.chi = up - self.cut_near * down
        self.ends = jnp.where(self.cell == 0, self.is_first, 0.0) + jnp.where(
            self.cell == self.m - 1, self.is_last, 0.0
        )
        self.weight = self.green * (self.rho + self.corner * self.ends)
        self.send_up = self.weight * self.chi * self.power(self.m - self.c)
        self.send_down = self.weight * self.phi * self.power(self.c - 1)
        self.get_up = self.phi * self.power(self.c)
        self.get_down = self.chi * self.power(self.m + 1 - self.c)
        self.head = jnp.where(self.cell == 0, 1.0, 0.0).astype(F32)
        self.tail = jnp.where(self.cell == self.m - 1, 1.0, 0.0).astype(F32)


def split(a):
    hi = a.astype(BF16)
    return hi, (a - hi.astype(F32)).astype(BF16)


def dot(a, b, ca, cb):
    return lax.dot_general(a, b, (((ca,), (cb,)), ((), ())), preferred_element_type=F32)


def moments_kernel(devices, rates, x, out, table, eighth, up_rows, down_rows, ends):
    step = pl.program_id(0)
    group, m = x.shape[0], x.shape[1]
    planes = table.shape[0]
    position = lax.axis_index("gy")

    @pl.when(step == 0)
    def _():
        spread(rates, table)
        eighth[...] = Line(table[...], position, devices, m).power(8)

    for g in range(group):
        k = step * group + g
        ratio = jnp.broadcast_to(eighth[pl.ds(k, 1), :], (8, x.shape[2]))
        up, down = x[g, 0:8, :], x[g, m - 8 : m, :]
        for v in range(1, m // 8):
            up = up * ratio + x[g, 8 * v : 8 * v + 8, :]
            w = m - 8 - 8 * v
            down = down * ratio + x[g, w : w + 8, :]
        up_rows[pl.ds(k, 1)] = up[None]
        down_rows[pl.ds(k, 1)] = down[None]
    ends[0, pl.ds(pl.multiple_of(step * group, group), group), :] = x[:, 0, :]
    ends[1, pl.ds(pl.multiple_of(step * group, group), group), :] = x[:, m - 1, :]

    @pl.when(step == pl.num_programs(0) - 1)
    def _():
        line = Line(table[...], position, devices, m)
        one = line.power(1)
        up, down = up_rows[:, 0, :], down_rows[:, 7, :]
        for s in range(1, 8):
            up = up * one + up_rows[:, s, :]
            down = down * one + down_rows[:, 7 - s, :]
        first, last = ends[0], ends[1]
        lower, upper = line.corner * line.is_first * first, line.corner * line.is_last * last
        across = line.power(m - 1)
        up = line.rho * up + across * lower + upper
        down = line.rho * down + lower + across * upper
        going_up = line.green * (up - line.power(2 * line.near + m + 1) * down)
        going_down = line.green * (down - line.power(2 * line.far - m - 1) * up)
        for d in range(devices):
            ahead = d > position
            out[d, :planes, :] = jnp.where(ahead, going_up, going_down)
            out[d, planes:, :] = jnp.where(ahead, last, first)


def columns(theta, cut_far, cut_near, m):
    shape = (8, theta.shape[1])
    i = (lax.broadcasted_iota(jnp.int32, shape, 0) + (1 - m // 2)).astype(F32)
    down, up = jnp.exp(-theta * i), jnp.exp(theta * i)
    grow, fall = jnp.exp(theta * 8.0), jnp.exp(theta * -8.0)
    phi, chi = [], []
    for _ in range(m // 8):
        phi.append(down - cut_far * up)
        chi.append(up - cut_near * down)
        down, up = down * fall, up * grow
    return phi, chi


def local_kernel(dev_y, dev_z, rates_y, rates_z, x, out, sums, table, ytab, ztab, nz, band):
    step = pl.program_id(0)
    group, m, n = x.shape
    pos_y, pos_z = lax.axis_index("gy"), lax.axis_index("gz")

    @pl.when(step == 0)
    def _():
        spread(rates_y, table)
        y = Line(table[...], pos_y, dev_y, m)
        y.vectors()
        for i, row in enumerate(
            (y.theta, y.cut_far, y.cut_near, y.phi * y.weight, y.chi * y.weight, y.mid, y.side)
        ):
            ytab[i] = row
        spread(rates_z, table)
        z = Line(table[...], pos_z, dev_z, n)
        z.vectors()
        base = z.green * z.rho
        for i, row in enumerate(
            (z.theta, z.cut_far, z.cut_near, z.phi * base, z.chi * base, z.mid, z.side, z.corner / z.rho)
        ):
            ztab[i] = row
        for i, row in enumerate((z.send_up, z.send_down, z.head, z.tail)):
            nz[:, i, :] = row
            nz[:, 4 + i, :] = jnp.zeros_like(row)
        r = lax.broadcasted_iota(jnp.int32, (m, n), 0)
        c = lax.broadcasted_iota(jnp.int32, (m, n), 1)
        band[0] = jnp.where(r == c, 1.0, 0.0)
        band[1] = jnp.where((r == c + 1) | (r + 1 == c), 1.0, 0.0)

    z_first = jnp.where(pos_z == 0, 1.0, 0.0).astype(F32)
    z_last = jnp.where(pos_z == dev_z - 1, 1.0, 0.0).astype(F32)
    sub = lax.broadcasted_iota(jnp.int32, (8, n), 0)
    at_head = jnp.where(sub == 0, z_first, 0.0)
    at_tail = jnp.where(sub == 7, z_last, 0.0)

    def one(g, carry):
        k = step * group + g

        def rows(ref, i):
            return ref[i, pl.ds(k, 1), :]

        phi, chi = columns(rows(ytab, 0), rows(ytab, 1), rows(ytab, 2), m)
        phi_row, chi_row, mid, side = [rows(ytab, i) for i in (3, 4, 5, 6)]
        dmat = jnp.concatenate(
            [
                jnp.minimum(phi[v] * chi_row, chi[v] * phi_row)
                + mid * band[0, 8 * v : 8 * v + 8, :]
                + side * band[1, 8 * v : 8 * v + 8, :]
                for v in range(m // 8)
            ],
            axis=0,
        )
        d_hi, d_lo = split(dmat)
        x_hi, x_lo = split(x[g])
        turned = dot(
            jnp.concatenate([d_hi, d_lo, d_hi], axis=1),
            jnp.concatenate([x_hi, x_hi, x_lo], axis=0),
            1,
            0,
        )
        t_hi, t_lo = split(turned)

        phi, chi = columns(rows(ztab, 0), rows(ztab, 1), rows(ztab, 2), n)
        phi_row, chi_row, mid, side, edge = [rows(ztab, i) for i in (3, 4, 5, 6, 7)]
        head, tail = 1.0 + edge * at_head, 1.0 + edge * at_tail
        phi[0], chi[0] = phi[0] * head, chi[0] * head
        phi[-1], chi[-1] = phi[-1] * tail, chi[-1] * tail
        bmat = jnp.concatenate(
            [
                jnp.minimum(phi[v] * chi_row, chi[v] * phi_row)
                + mid * band[0, 8 * v : 8 * v + 8, :]
                + side * band[1, 8 * v : 8 * v + 8, :]
                for v in range(n // 8)
            ],
            axis=0,
        )
        b_hi, b_lo = split(bmat)
        out[g] = dot(
            jnp.concatenate([t_hi, t_lo, t_hi], axis=1),
            jnp.concatenate([b_hi, b_hi, b_lo], axis=0),
            1,
            0,
        )
        functionals = nz[pl.ds(k, 1)][0]
        f_hi = functionals.astype(BF16).astype(F32)
        f16 = jnp.concatenate([f_hi, functionals - f_hi], axis=0).astype(BF16)
        both = dot(f16, t_hi, 1, 1) + dot(f16, t_lo, 1, 1)
        sums[g] = both[:8] + both[8:]
        return carry

    lax.fori_loop(0, group, one, 0)


def along_lanes(line, f):
    m = line.m
    cell = line.cell
    near = 1.0 - line.power(2 * line.near) * jnp.exp(-2.0 * line.theta * (cell + 1).astype(F32))
    far = 1.0 - line.power(2 * (line.far - m - 1)) * jnp.exp(
        -2.0 * line.theta * (m - cell).astype(F32)
    )
    ups, downs = [], []
    span = 1
    while span < m:
        ratio = line.power(span)
        ups.append((span, jnp.where(cell >= span, ratio, 0.0)))
        downs.append((m - span, jnp.where(cell < m - span, ratio, 0.0)))
        span *= 2
    results = []
    for v in f:
        source = line.weight * v
        up, start = near * source, far * source
        for shift, ratio in ups:
            up = up + ratio * pltpu.roll(up, shift, 1)
        down = start
        for shift, ratio in downs:
            down = down + ratio * pltpu.roll(down, shift, 1)
        down = down - start
        left, right = pltpu.roll(v, 1, 1), pltpu.roll(v, m - 1, 1)
        left = jnp.where(cell > 0, left, 0.0)
        right = jnp.where(cell < m - 1, right, 0.0)
        results.append(far * up + near * down + line.mid * v + line.side * (left + right))
    return results


def incoming(ref, position, devices, reach, pick):
    up = jnp.zeros_like(reach)
    down = jnp.zeros_like(reach)
    for d in range(devices):
        up = jnp.where(d < position, up * reach + pick(d, 0), up)
        e = devices - 1 - d
        down = jnp.where(e > position, down * reach + pick(e, 1), down)
    return up, down


def middle_kernel(dev_y, dev_z, rates_y, rates_z, got, sums, send, held, table):
    planes, n = table.shape
    m = sums.shape[2]
    pos_y, pos_z = lax.axis_index("gy"), lax.axis_index("gz")
    spread(rates_y, table)
    y = Line(table[...], pos_y, dev_y, m)
    y.vectors()
    up, down = incoming(got, pos_y, dev_y, y.power(m), lambda d, kind: got[d, :planes, :])
    before = got[pl.ds(jnp.maximum(pos_y - 1, 0), 1), pl.ds(planes, planes), :][0]
    after = got[pl.ds(jnp.minimum(pos_y + 1, dev_y - 1), 1), pl.ds(planes, planes), :][0]
    before = jnp.where(pos_y > 0, before, 0.0)
    after = jnp.where(pos_y < dev_y - 1, after, 0.0)
    spread(rates_z, table)
    z = Line(table[...], pos_z, dev_z, n)
    z.vectors()
    arrivals = (up, down, before, after)
    places = (y.get_up, y.get_down, y.side * y.head, y.side * y.tail)
    for kind, functional in enumerate((z.send_up, z.send_down, z.head, z.tail)):
        total = sums[:, kind, :]
        for place, arrival in zip(places, arrivals):
            total = total + place * jnp.sum(arrival * functional, axis=1, keepdims=True)
        send[kind] = total
    for i, row in enumerate(along_lanes(z, arrivals)):
        held[i] = row


def final_kernel(dev_y, dev_z, rates_y, rates_z, local, held, got, out, table, left, right):
    step = pl.program_id(0)
    group, m, n = local.shape
    planes = table.shape[0]
    pos_y, pos_z = lax.axis_index("gy"), lax.axis_index("gz")

    @pl.when(step == 0)
    def _():
        spread(rates_y, table)
        y = Line(table[...], pos_y, dev_y, m)
        y.vectors()
        for i, row in enumerate((y.get_up, y.get_down, y.side * y.head, y.side * y.tail)):
            left[:, i, :] = row
            right[:, i, :] = held[i]
        spread(rates_z, table)
        z = Line(table[...], pos_z, dev_z, n)
        z.vectors()
        up, down = incoming(got, pos_z, dev_z, z.power(n), lambda d, kind: got[d, kind])
        before = got[pl.ds(jnp.maximum(pos_z - 1, 0), 1), 3][0]
        after = got[pl.ds(jnp.minimum(pos_z + 1, dev_z - 1), 1), 2][0]
        before = jnp.where(pos_z > 0, before, 0.0)
        after = jnp.where(pos_z < dev_z - 1, after, 0.0)
        for i, row in enumerate((up, down, before, after)):
            left[:, 4 + i, :] = row
        for i, row in enumerate((z.get_up, z.get_down, z.side * z.head, z.side * z.tail)):
            right[:, 4 + i, :] = row

    for g in range(group):
        k = step * group + g
        a, b = left[pl.ds(k, 1)][0], right[pl.ds(k, 1)][0]
        a_hi, b_hi = a.astype(BF16).astype(F32), b.astype(BF16).astype(F32)
        a_lo, b_lo = a - a_hi, b - b_hi
        a = jnp.concatenate([a_hi, a_lo, a_hi, a_lo], axis=0).astype(BF16)
        b = jnp.concatenate([b_hi, b_hi, b_lo, b_lo], axis=0).astype(BF16)
        out[g] = local[g] + dot(a, b, 0, 0)


def per_device(x, rates_y, rates_z):
    planes, m, n = x.shape
    dev_y, dev_z = lax.axis_size("gy"), lax.axis_size("gz")
    group = planes // STEPS
    smem = pl.BlockSpec(memory_space=pltpu.SMEM)
    whole = pl.BlockSpec(memory_space=pltpu.VMEM)
    slab = pl.BlockSpec((group, m, n), lambda i: (i, 0, 0))

    def params():
        return pltpu.CompilerParams(vmem_limit_bytes=VMEM)

    def cost(flops, moved):
        return pl.CostEstimate(flops=flops, bytes_accessed=moved, transcendentals=0)

    def shape(*dims):
        return jax.ShapeDtypeStruct(dims, F32)

    cells = planes * m * n
    payload = pl.pallas_call(
        functools.partial(moments_kernel, dev_y),
        grid=(STEPS,),
        in_specs=[smem, slab],
        out_specs=pl.BlockSpec((dev_y, 2 * planes, n), lambda i: (0, 0, 0)),
        out_shape=shape(dev_y, 2 * planes, n),
        scratch_shapes=[
            pltpu.VMEM((planes, n), F32),
            pltpu.VMEM((planes, n), F32),
            pltpu.VMEM((planes, 8, n), F32),
            pltpu.VMEM((planes, 8, n), F32),
            pltpu.VMEM((2, planes, n), F32),
        ],
        compiler_params=params(),
        cost_estimate=cost(4 * cells, 4 * cells),
        name="moments",
    )(rates_y, x)
    got_y = lax.all_to_all(payload, "gy", 0, 0, tiled=True)
    local, sums = pl.pallas_call(
        functools.partial(local_kernel, dev_y, dev_z),
        grid=(STEPS,),
        in_specs=[smem, smem, slab],
        out_specs=[slab, pl.BlockSpec((group, 8, m), lambda i: (i, 0, 0))],
        out_shape=[shape(planes, m, n), shape(planes, 8, m)],
        scratch_shapes=[
            pltpu.VMEM((planes, n), F32),
            pltpu.VMEM((7, planes, m), F32),
            pltpu.VMEM((8, planes, n), F32),
            pltpu.VMEM((planes, 8, n), F32),
            pltpu.VMEM((2, m, n), F32),
        ],
        compiler_params=params(),
        cost_estimate=cost(12 * cells * m, 8 * cells),
        name="local",
    )(rates_y, rates_z, x)
    send, held = pl.pallas_call(
        functools.partial(middle_kernel, dev_y, dev_z),
        in_specs=[smem, smem, whole, whole],
        out_specs=[whole, whole],
        out_shape=[shape(4, planes, m), shape(4, planes, n)],
        scratch_shapes=[pltpu.VMEM((planes, n), F32)],
        compiler_params=params(),
        cost_estimate=cost(planes * n * 400, planes * n * 100),
        name="middle",
    )(rates_y, rates_z, got_y, sums)
    got_z = lax.all_gather(send, "gz", axis=0, tiled=False)
    return pl.pallas_call(
        functools.partial(final_kernel, dev_y, dev_z),
        grid=(STEPS,),
        in_specs=[smem, smem, slab, whole, whole],
        out_specs=slab,
        out_shape=shape(planes, m, n),
        scratch_shapes=[
            pltpu.VMEM((planes, n), F32),
            pltpu.VMEM((planes, 8, m), F32),
            pltpu.VMEM((planes, 8, n), F32),
        ],
        compiler_params=params(),
        cost_estimate=cost(64 * cells, 8 * cells),
        name="final",
    )(rates_y, rates_z, local, held, got_z)


def solution(mesh):
    return jax.shard_map(
        per_device,
        mesh=mesh,
        in_specs=(P(None, "gy", "gz"), P(), P()),
        out_specs=P(None, "gy", "gz"),
        check_vma=False,
    )
```

```python
import functools

import jax
import jax.numpy as jnp
from jax import lax
from jax.experimental import pallas as pl
from jax.experimental.pallas import tpu as pltpu
from jax.sharding import PartitionSpec as P

alpha = 2.0 / 11.0
inner_weight = 12.0 / 11.0
outer_weight = 3.0 / 44.0
F32 = jnp.float32
BF16 = jnp.bfloat16
STEPS = 4
VMEM = 24 * 1024 * 1024
LOCALV = 24
FINALV = 24


def spread(rates, table):
    for k in range(table.shape[0]):
        table[pl.ds(k, 1), :] = jnp.full((1, table.shape[1]), rates[k], F32)


class Line:
    def __init__(self, rate, position, devices, m):
        beside = inner_weight * rate - alpha
        eps = (1.0 + 2.0 * alpha) / (2.0 * beside)
        sinh = jnp.sqrt(eps * (2.0 + eps))
        corner = rate * outer_weight
        self.m = m
        self.theta = jnp.log1p(eps + sinh)
        total = m * devices
        self.far = total + 1 - m * position
        self.near = m * position
        self.c = m // 2
        self.green = 1.0 / (2.0 * beside * sinh * (1.0 - self.power(2 * (total + 1))))
        self.rho = 1.0 + 2.0 * alpha * (1.0 + eps) + 4.0 * corner * eps * (2.0 + eps)
        self.side = -corner / beside
        self.mid = 2.0 * self.side * (1.0 + eps) - alpha / beside
        self.corner = corner
        self.is_first = jnp.where(position == 0, 1.0, 0.0).astype(F32)
        self.is_last = jnp.where(position == devices - 1, 1.0, 0.0).astype(F32)
        self.cell = lax.broadcasted_iota(jnp.int32, rate.shape, 1)

    def power(self, n):
        return jnp.exp(-self.theta * jnp.asarray(n, F32))

    def vectors(self):
        i = (self.cell + (1 - self.c)).astype(F32)
        down, up = jnp.exp(-self.theta * i), jnp.exp(self.theta * i)
        self.cut_far = self.power(2 * (self.far - self.c))
        self.cut_near = self.power(2 * (self.near + self.c))
        self.phi = down - self.cut_far * up
        self.chi = up - self.cut_near * down
        self.ends = jnp.where(self.cell == 0, self.is_first, 0.0) + jnp.where(
            self.cell == self.m - 1, self.is_last, 0.0
        )
        self.weight = self.green * (self.rho + self.corner * self.ends)
        self.send_up = self.weight * self.chi * self.power(self.m - self.c)
        self.send_down = self.weight * self.phi * self.power(self.c - 1)
        self.get_up = self.phi * self.power(self.c)
        self.get_down = self.chi * self.power(self.m + 1 - self.c)
        self.head = jnp.where(self.cell == 0, 1.0, 0.0).astype(F32)
        self.tail = jnp.where(self.cell == self.m - 1, 1.0, 0.0).astype(F32)


def split(a):
    hi = a.astype(BF16)
    return hi, (a - hi.astype(F32)).astype(BF16)


def dot(a, b, ca, cb):
    return lax.dot_general(a, b, (((ca,), (cb,)), ((), ())), preferred_element_type=F32)


def product(a_hi, a_lo, b_hi, b_lo):
    b = jnp.concatenate([b_hi, b_lo], axis=1)
    n = b_hi.shape[1]
    both = dot(jnp.concatenate([a_hi, a_lo], axis=1), jnp.concatenate([b, b], axis=0), 1, 0)
    return both[:, :n] + both[:, n:]


def moments_kernel(
    devices, rates_hbm, x_hbm, out, rates, x, rate_sem, x_sems, table, up_rows, down_rows
):
    planes, m, n = x.shape
    parts = x_sems.shape[0]
    group = planes // parts
    position = lax.axis_index("gy")
    rate_copy = pltpu.make_async_copy(rates_hbm, rates, rate_sem)
    rate_copy.start()
    copies = []
    for i in range(parts):
        some = pl.ds(i * group, group)
        copies.append(pltpu.make_async_copy(x_hbm.at[some], x.at[some], x_sems.at[i]))
        copies[i].start()
    rate_copy.wait()
    spread(rates, table)
    line = Line(table[...], position, devices, m)
    one = line.power(1)
    eighth = line.power(8)
    across = line.power(m - 1)
    lower_scale, upper_scale = line.corner * line.is_first, line.corner * line.is_last
    turn_up, turn_down = line.power(2 * line.near + m + 1), line.power(2 * line.far - m - 1)
    table[...] = eighth
    for i in range(parts):
        copies[i].wait()
        for k in range(i * group, i * group + group):
            ratio = jnp.broadcast_to(table[k : k + 1, :], (8, n))
            up, down = x[k, 0:8, :], x[k, m - 8 : m, :]
            for v in range(1, m // 8):
                up = up * ratio + x[k, 8 * v : 8 * v + 8, :]
                w = m - 8 - 8 * v
                down = down * ratio + x[k, w : w + 8, :]
            up_rows[k] = up
            down_rows[k] = down
    up, down = up_rows[:, 0, :], down_rows[:, 7, :]
    for s in range(1, 8):
        up = up * one + up_rows[:, s, :]
        down = down * one + down_rows[:, 7 - s, :]
    first, last = x[:, 0, :], x[:, m - 1, :]
    lower, upper = lower_scale * first, upper_scale * last
    up = line.rho * up + across * lower + upper
    down = line.rho * down + lower + across * upper
    going_up = line.green * (up - turn_up * down)
    going_down = line.green * (down - turn_down * up)
    for d in range(devices):
        ahead = d > position
        out[d, :planes, :] = jnp.where(ahead, going_up, going_down)
        out[d, planes:, :] = jnp.where(ahead, last, first)


def columns(theta, cut_far, cut_near, m):
    shape = (8, theta.shape[1])
    i = (lax.broadcasted_iota(jnp.int32, shape, 0) + (1 - m // 2)).astype(F32)
    down, up = jnp.exp(-theta * i), jnp.exp(theta * i)
    grow, fall = jnp.exp(theta * 8.0), jnp.exp(theta * -8.0)
    phi, chi = [], []
    for _ in range(m // 8):
        phi.append(down - cut_far * up)
        chi.append(up - cut_near * down)
        down, up = down * fall, up * grow
    return phi, chi


def local_kernel(
    dev_y, dev_z, rates_y, rates_z, x, out, sums, ykeep, zkeep, table, ytab, ztab, nz, band
):
    step = pl.program_id(0)
    group, m, n = x.shape
    pos_y, pos_z = lax.axis_index("gy"), lax.axis_index("gz")

    @pl.when(step == 0)
    def _():
        spread(rates_y, table)
        y = Line(table[...], pos_y, dev_y, m)
        y.vectors()
        for i, row in enumerate(
            (y.theta, y.cut_far, y.cut_near, y.phi * y.weight, y.chi * y.weight, y.mid, y.side)
        ):
            ytab[i] = row
        for i, row in enumerate((y.get_up, y.get_down, y.side * y.head, y.side * y.tail, y.power(m))):
            ykeep[i] = row
        spread(rates_z, table)
        z = Line(table[...], pos_z, dev_z, n)
        z.vectors()
        base = z.green * z.rho
        for i, row in enumerate(
            (z.theta, z.cut_far, z.cut_near, z.phi * base, z.chi * base, z.mid, z.side, z.corner / z.rho)
        ):
            ztab[i] = row
        for i, row in enumerate(
            (z.get_up, z.get_down, z.side * z.head, z.side * z.tail, z.power(n), z.send_up, z.send_down)
        ):
            zkeep[i] = row
        for i, row in enumerate((z.send_up, z.send_down, z.head, z.tail)):
            nz[:, i, :] = row
            nz[:, 4 + i, :] = jnp.zeros_like(row)
        r = lax.broadcasted_iota(jnp.int32, (m, n), 0)
        c = lax.broadcasted_iota(jnp.int32, (m, n), 1)
        band[0] = jnp.where(r == c, 1.0, 0.0)
        band[1] = jnp.where((r == c + 1) | (r + 1 == c), 1.0, 0.0)

    z_first = jnp.where(pos_z == 0, 1.0, 0.0).astype(F32)
    z_last = jnp.where(pos_z == dev_z - 1, 1.0, 0.0).astype(F32)
    sub = lax.broadcasted_iota(jnp.int32, (8, n), 0)
    at_head = jnp.where(sub == 0, z_first, 0.0)
    at_tail = jnp.where(sub == 7, z_last, 0.0)

    def one(g, carry):
        k = step * group + g

        def rows(ref, i):
            return ref[i, pl.ds(k, 1), :]

        phi, chi = columns(rows(ytab, 0), rows(ytab, 1), rows(ytab, 2), m)
        phi_row, chi_row, mid, side = [rows(ytab, i) for i in (3, 4, 5, 6)]
        dmat = jnp.concatenate(
            [
                jnp.minimum(phi[v] * chi_row, chi[v] * phi_row)
                + mid * band[0, 8 * v : 8 * v + 8, :]
                + side * band[1, 8 * v : 8 * v + 8, :]
                for v in range(m // 8)
            ],
            axis=0,
        )
        d_hi, d_lo = split(dmat)
        x_hi, x_lo = split(x[g])
        turned = product(d_hi, d_lo, x_hi, x_lo)
        t_hi, t_lo = split(turned)

        phi, chi = columns(rows(ztab, 0), rows(ztab, 1), rows(ztab, 2), n)
        phi_row, chi_row, mid, side, edge = [rows(ztab, i) for i in (3, 4, 5, 6, 7)]
        head, tail = 1.0 + edge * at_head, 1.0 + edge * at_tail
        phi[0], chi[0] = phi[0] * head, chi[0] * head
        phi[-1], chi[-1] = phi[-1] * tail, chi[-1] * tail
        bmat = jnp.concatenate(
            [
                jnp.minimum(phi[v] * chi_row, chi[v] * phi_row)
                + mid * band[0, 8 * v : 8 * v + 8, :]
                + side * band[1, 8 * v : 8 * v + 8, :]
                for v in range(n // 8)
            ],
            axis=0,
        )
        b_hi, b_lo = split(bmat)
        out[g] = product(t_hi, t_lo, b_hi, b_lo)
        functionals = nz[pl.ds(k, 1)][0]
        f_hi = functionals.astype(BF16).astype(F32)
        f16 = jnp.concatenate([f_hi, functionals - f_hi], axis=0).astype(BF16)
        both = dot(
            jnp.concatenate([f16, f16], axis=1), jnp.concatenate([t_hi, t_lo], axis=1), 1, 1
        )
        sums[g] = both[:8] + both[8:]
        return carry

    lax.fori_loop(0, group, one, 0, unroll=True)


def along_lanes(line, f):
    m = line.m
    cell = line.cell
    near = 1.0 - line.power(2 * line.near) * jnp.exp(-2.0 * line.theta * (cell + 1).astype(F32))
    far = 1.0 - line.power(2 * (line.far - m - 1)) * jnp.exp(
        -2.0 * line.theta * (m - cell).astype(F32)
    )
    ups, downs = [], []
    span = 1
    while span < m:
        ratio = line.power(span)
        ups.append((span, jnp.where(cell >= span, ratio, 0.0)))
        downs.append((m - span, jnp.where(cell < m - span, ratio, 0.0)))
        span *= 2
    results = []
    for v in f:
        source = line.weight * v
        up, start = near * source, far * source
        for shift, ratio in ups:
            up = up + ratio * pltpu.roll(up, shift, 1)
        down = start
        for shift, ratio in downs:
            down = down + ratio * pltpu.roll(down, shift, 1)
        down = down - start
        left, right = pltpu.roll(v, 1, 1), pltpu.roll(v, m - 1, 1)
        left = jnp.where(cell > 0, left, 0.0)
        right = jnp.where(cell < m - 1, right, 0.0)
        results.append(far * up + near * down + line.mid * v + line.side * (left + right))
    return results


def incoming(ref, position, devices, reach, pick):
    up = jnp.zeros_like(reach)
    down = jnp.zeros_like(reach)
    for d in range(devices):
        up = jnp.where(d < position, up * reach + pick(d, 0), up)
        e = devices - 1 - d
        down = jnp.where(e > position, down * reach + pick(e, 1), down)
    return up, down


def arrivals(dev_y, reach, got):
    planes = reach.shape[0]
    position = lax.axis_index("gy")
    up, down = incoming(got, position, dev_y, reach, lambda d, kind: got[d, :planes, :])
    before = got[pl.ds(jnp.maximum(position - 1, 0), 1), pl.ds(planes, planes), :][0]
    after = got[pl.ds(jnp.minimum(position + 1, dev_y - 1), 1), pl.ds(planes, planes), :][0]
    before = jnp.where(position > 0, before, 0.0)
    after = jnp.where(position < dev_y - 1, after, 0.0)
    return up, down, before, after


def middle_kernel(dev_y, dev_z, got, sums, ykeep, zkeep, *sends):
    pos_z = lax.axis_index("gz")
    n = zkeep.shape[2]
    rows = arrivals(dev_y, ykeep[4], got)
    totals = []
    for kind in range(4):
        total = sums[:, kind, :]
        for i, row in enumerate(rows):
            if kind < 2:
                amount = jnp.sum(row * zkeep[5 + kind], axis=1, keepdims=True)
            else:
                amount = row[:, :1] if kind == 2 else row[:, n - 1 :]
            total = total + ykeep[i] * amount
        totals.append(total)
    up, down, head, tail = totals
    for by, send in enumerate(sends):
        ahead = pos_z + by + 1 < dev_z
        send[0] = jnp.where(ahead, up, down)
        send[1] = jnp.where(ahead, tail, head)


def held_kernel(dev_y, dev_z, rates_z, got, ykeep, held, table):
    spread(rates_z, table)
    z = Line(table[...], lax.axis_index("gz"), dev_z, table.shape[1])
    z.vectors()
    for i, row in enumerate(along_lanes(z, arrivals(dev_y, ykeep[4], got))):
        held[i] = row


def final_kernel(dev_z, local_hbm, held, ykeep, zkeep, *rest):
    gots, rest = rest[: dev_z - 1], rest[dev_z - 1 :]
    out_hbm, local, out, in_sems, out_sems, left, right = rest
    planes, m, n = local.shape
    parts = in_sems.shape[0]
    group = planes // parts
    pos_z = lax.axis_index("gz")
    loads, stores = [], []
    for i in range(parts):
        some = pl.ds(i * group, group)
        loads.append(pltpu.make_async_copy(local_hbm.at[some], local.at[some], in_sems.at[i]))
        stores.append(pltpu.make_async_copy(out.at[some], out_hbm.at[some], out_sems.at[i]))
        loads[i].start()
    for i in range(4):
        left[:, i, :] = ykeep[i]
        right[:, i, :] = held[i]
        right[:, 4 + i, :] = zkeep[i]
    reach = zkeep[4]
    up, down = jnp.zeros_like(gots[0][0]), jnp.zeros_like(gots[0][0])
    scale = jnp.ones_like(reach)
    for by in range(dev_z - 1):
        up = up + jnp.where(pos_z > by, scale * gots[by][0], 0.0)
        behind = gots[dev_z - 2 - by]
        down = down + jnp.where(pos_z + by + 1 < dev_z, scale * behind[0], 0.0)
        scale = scale * reach
    left[:, 4, :] = up
    left[:, 5, :] = down
    left[:, 6, :] = jnp.where(pos_z > 0, gots[0][1], 0.0)
    left[:, 7, :] = jnp.where(pos_z < dev_z - 1, gots[-1][1], 0.0)

    for i in range(parts):
        loads[i].wait()
        for k in range(i * group, i * group + group):
            a, b = left[k], right[k]
            a_hi, b_hi = a.astype(BF16).astype(F32), b.astype(BF16).astype(F32)
            a_lo, b_lo = a - a_hi, b - b_hi
            a = jnp.concatenate([a_hi, a_lo, a_hi, a_lo], axis=0).astype(BF16)
            b = jnp.concatenate([b_hi, b_hi, b_lo, b_lo], axis=0).astype(BF16)
            out[k] = local[k] + dot(a, b, 0, 0)
        stores[i].start()
    for i in range(parts):
        stores[i].wait()


def per_device(x, rates_y, rates_z):
    planes, m, n = x.shape
    dev_y, dev_z = lax.axis_size("gy"), lax.axis_size("gz")
    group = planes // STEPS
    smem = pl.BlockSpec(memory_space=pltpu.SMEM)
    whole = pl.BlockSpec(memory_space=pltpu.VMEM)
    slab = pl.BlockSpec((group, m, n), lambda i: (i, 0, 0))

    def params():
        return pltpu.CompilerParams(vmem_limit_bytes=VMEM)

    def cost(flops, moved):
        return pl.CostEstimate(flops=flops, bytes_accessed=moved, transcendentals=0)

    def shape(*dims):
        return jax.ShapeDtypeStruct(dims, F32)

    cells = planes * m * n
    hbm = pl.BlockSpec(memory_space=pltpu.HBM)
    payload = pl.pallas_call(
        functools.partial(moments_kernel, dev_y),
        in_specs=[hbm, hbm],
        out_specs=whole,
        out_shape=shape(dev_y, 2 * planes, n),
        scratch_shapes=[
            pltpu.SMEM((planes,), F32),
            pltpu.VMEM((planes, m, n), F32),
            pltpu.SemaphoreType.DMA,
            pltpu.SemaphoreType.DMA((8,)),
            pltpu.VMEM((planes, n), F32),
            pltpu.VMEM((planes, 8, n), F32),
            pltpu.VMEM((planes, 8, n), F32),
        ],
        compiler_params=pltpu.CompilerParams(vmem_limit_bytes=60 * 1024 * 1024),
        cost_estimate=cost(4 * cells, 4 * cells),
        name="moments",
    )(rates_y, x)
    got_y = lax.all_to_all(payload, "gy", 0, 0, tiled=True)
    def full(*dims):
        return pl.BlockSpec(dims, lambda i: (0,) * len(dims))

    local, sums, ykeep, zkeep = pl.pallas_call(
        functools.partial(local_kernel, dev_y, dev_z),
        grid=(STEPS,),
        in_specs=[smem, smem, slab],
        out_specs=[
            slab,
            pl.BlockSpec((group, 8, m), lambda i: (i, 0, 0)),
            full(5, planes, m),
            full(7, planes, n),
        ],
        out_shape=[
            shape(planes, m, n),
            shape(planes, 8, m),
            shape(5, planes, m),
            shape(7, planes, n),
        ],
        scratch_shapes=[
            pltpu.VMEM((planes, n), F32),
            pltpu.VMEM((7, planes, m), F32),
            pltpu.VMEM((8, planes, n), F32),
            pltpu.VMEM((planes, 8, n), F32),
            pltpu.VMEM((2, m, n), F32),
        ],
        compiler_params=pltpu.CompilerParams(vmem_limit_bytes=LOCALV * 1024 * 1024),
        cost_estimate=cost(12 * cells * m, 8 * cells),
        name="local",
    )(rates_y, rates_z, x)
    sends = pl.pallas_call(
        functools.partial(middle_kernel, dev_y, dev_z),
        in_specs=[whole] * 4,
        out_specs=[whole] * (dev_z - 1),
        out_shape=[shape(2, planes, m)] * (dev_z - 1),
        compiler_params=params(),
        cost_estimate=cost(planes * n * 100, planes * n * 100),
        name="middle",
    )(got_y, sums, ykeep, zkeep)
    got_z = [
        lax.ppermute(send, "gz", [(i, (i + by + 1) % dev_z) for i in range(dev_z)])
        for by, send in enumerate(sends)
    ]
    held = pl.pallas_call(
        functools.partial(held_kernel, dev_y, dev_z),
        in_specs=[smem, whole, whole],
        out_specs=whole,
        out_shape=shape(4, planes, n),
        scratch_shapes=[pltpu.VMEM((planes, n), F32)],
        compiler_params=params(),
        cost_estimate=cost(planes * n * 400, planes * n * 100),
        name="held",
    )(rates_z, got_y, ykeep)
    return pl.pallas_call(
        functools.partial(final_kernel, dev_z),
        in_specs=[hbm] + [whole] * (dev_z + 2),
        out_specs=hbm,
        out_shape=shape(planes, m, n),
        input_output_aliases={0: 0},
        scratch_shapes=[
            pltpu.VMEM((planes, m, n), F32),
            pltpu.VMEM((planes, m, n), F32),
            pltpu.SemaphoreType.DMA((4,)),
            pltpu.SemaphoreType.DMA((4,)),
            pltpu.VMEM((planes, 8, m), F32),
            pltpu.VMEM((planes, 8, n), F32),
        ],
        compiler_params=pltpu.CompilerParams(vmem_limit_bytes=FINALV * 1024 * 1024),
        cost_estimate=cost(64 * cells, 8 * cells),
        name="final",
    )(local, held, ykeep, zkeep, *got_z)


def solution(mesh):
    return jax.shard_map(
        per_device,
        mesh=mesh,
        in_specs=(P(None, "gy", "gz"), P(), P()),
        out_specs=P(None, "gy", "gz"),
        check_vma=False,
    )
```

```python
import functools

import jax
import jax.numpy as jnp
from jax import lax
from jax.experimental import pallas as pl
from jax.experimental.pallas import tpu as pltpu
from jax.sharding import PartitionSpec as P

alpha = 2.0 / 11.0
inner_weight = 12.0 / 11.0
outer_weight = 3.0 / 44.0
F32 = jnp.float32
BF16 = jnp.bfloat16
VMEM = 24 * 1024 * 1024
MOMV = 60


def spread(rates, table):
    for k in range(table.shape[0]):
        table[pl.ds(k, 1), :] = jnp.full((1, table.shape[1]), rates[k], F32)


class Line:
    def __init__(self, rate, position, devices, m):
        beside = inner_weight * rate - alpha
        eps = (1.0 + 2.0 * alpha) / (2.0 * beside)
        sinh = jnp.sqrt(eps * (2.0 + eps))
        corner = rate * outer_weight
        self.m = m
        self.theta = jnp.log1p(eps + sinh)
        total = m * devices
        self.far = total + 1 - m * position
        self.near = m * position
        self.c = m // 2
        self.green = 1.0 / (2.0 * beside * sinh * (1.0 - self.power(2 * (total + 1))))
        self.rho = 1.0 + 2.0 * alpha * (1.0 + eps) + 4.0 * corner * eps * (2.0 + eps)
        self.side = -corner / beside
        self.mid = 2.0 * self.side * (1.0 + eps) - alpha / beside
        self.corner = corner
        self.is_first = jnp.where(position == 0, 1.0, 0.0).astype(F32)
        self.is_last = jnp.where(position == devices - 1, 1.0, 0.0).astype(F32)
        self.cell = lax.broadcasted_iota(jnp.int32, rate.shape, 1)

    def power(self, n):
        return jnp.exp(-self.theta * jnp.asarray(n, F32))

    def vectors(self):
        i = (self.cell + (1 - self.c)).astype(F32)
        down, up = jnp.exp(-self.theta * i), jnp.exp(self.theta * i)
        self.cut_far = self.power(2 * (self.far - self.c))
        self.cut_near = self.power(2 * (self.near + self.c))
        self.phi = down - self.cut_far * up
        self.chi = up - self.cut_near * down
        self.ends = jnp.where(self.cell == 0, self.is_first, 0.0) + jnp.where(
            self.cell == self.m - 1, self.is_last, 0.0
        )
        self.weight = self.green * (self.rho + self.corner * self.ends)
        self.send_up = self.weight * self.chi * self.power(self.m - self.c)
        self.send_down = self.weight * self.phi * self.power(self.c - 1)
        self.get_up = self.phi * self.power(self.c)
        self.get_down = self.chi * self.power(self.m + 1 - self.c)
        self.head = jnp.where(self.cell == 0, 1.0, 0.0).astype(F32)
        self.tail = jnp.where(self.cell == self.m - 1, 1.0, 0.0).astype(F32)


def split(a):
    hi = a.astype(BF16)
    return hi, (a - hi.astype(F32)).astype(BF16)


def dot(a, b, ca, cb):
    return lax.dot_general(a, b, (((ca,), (cb,)), ((), ())), preferred_element_type=F32)


def product(a_hi, a_lo, b_hi, b_lo):
    b = jnp.concatenate([b_hi, b_lo], axis=1)
    n = b_hi.shape[1]
    both = dot(jnp.concatenate([a_hi, a_lo], axis=1), jnp.concatenate([b, b], axis=0), 1, 0)
    return both[:, :n] + both[:, n:]


def moments_kernel(
    devices, rates_hbm, x_hbm, out, rates, x, rate_sem, x_sems, table, up_rows, down_rows
):
    planes, m, n = x.shape
    parts = x_sems.shape[0]
    group = planes // parts
    position = lax.axis_index("gy")
    rate_copy = pltpu.make_async_copy(rates_hbm, rates, rate_sem)
    rate_copy.start()
    copies = []
    for i in range(parts):
        some = pl.ds(i * group, group)
        copies.append(pltpu.make_async_copy(x_hbm.at[some], x.at[some], x_sems.at[i]))
        copies[i].start()
    rate_copy.wait()
    spread(rates, table)
    line = Line(table[...], position, devices, m)
    one = line.power(1)
    eighth = line.power(8)
    across = line.power(m - 1)
    lower_scale, upper_scale = line.corner * line.is_first, line.corner * line.is_last
    turn_up, turn_down = line.power(2 * line.near + m + 1), line.power(2 * line.far - m - 1)
    table[...] = eighth
    for i in range(parts):
        copies[i].wait()
        for k in range(i * group, i * group + group):
            ratio = jnp.broadcast_to(table[k : k + 1, :], (8, n))
            up, down = x[k, 0:8, :], x[k, m - 8 : m, :]
            for v in range(1, m // 8):
                up = up * ratio + x[k, 8 * v : 8 * v + 8, :]
                w = m - 8 - 8 * v
                down = down * ratio + x[k, w : w + 8, :]
            up_rows[k] = up
            down_rows[k] = down
    up, down = up_rows[:, 0, :], down_rows[:, 7, :]
    for s in range(1, 8):
        up = up * one + up_rows[:, s, :]
        down = down * one + down_rows[:, 7 - s, :]
    first, last = x[:, 0, :], x[:, m - 1, :]
    lower, upper = lower_scale * first, upper_scale * last
    up = line.rho * up + across * lower + upper
    down = line.rho * down + lower + across * upper
    going_up = line.green * (up - turn_up * down)
    going_down = line.green * (down - turn_down * up)
    out[0] = going_up
    out[1] = going_down
    out[2] = first
    out[3] = last


def columns(theta, cut_far, cut_near, m):
    shape = (8, theta.shape[1])
    i = (lax.broadcasted_iota(jnp.int32, shape, 0) + (1 - m // 2)).astype(F32)
    down, up = jnp.exp(-theta * i), jnp.exp(theta * i)
    grow, fall = jnp.exp(theta * 8.0), jnp.exp(theta * -8.0)
    phi, chi = [], []
    for _ in range(m // 8):
        phi.append(down - cut_far * up)
        chi.append(up - cut_near * down)
        down, up = down * fall, up * grow
    return phi, chi


def make_tables(dev_y, dev_z, rates_y, rates_z, m, n, ykeep, zkeep, ytab, ztab, nz, table):
    pos_y, pos_z = lax.axis_index("gy"), lax.axis_index("gz")
    spread(rates_y, table)
    y = Line(table[...], pos_y, dev_y, m)
    y.vectors()
    for i, row in enumerate((y.get_up, y.get_down, y.side * y.head, y.side * y.tail, y.theta)):
        ykeep[i] = row
    for i, row in enumerate(
        (y.theta, y.cut_far, y.cut_near, y.phi * y.weight, y.chi * y.weight, y.mid, y.side)
    ):
        ytab[i] = row
    spread(rates_z, table)
    z = Line(table[...], pos_z, dev_z, n)
    z.vectors()
    for i, row in enumerate(
        (z.get_up, z.get_down, z.side * z.head, z.side * z.tail, z.power(n), z.send_up, z.send_down)
    ):
        zkeep[i] = row
    base = z.green * z.rho
    for i, row in enumerate(
        (z.theta, z.cut_far, z.cut_near, z.phi * base, z.chi * base, z.mid, z.side, z.corner / z.rho)
    ):
        ztab[i] = row
    for i, row in enumerate((z.send_up, z.send_down, z.head, z.tail)):
        nz[:, i, :] = row
        nz[:, 4 + i, :] = jnp.zeros_like(row)


def local_kernel(dev_y, dev_z, lo, hi, *refs):
    if lo == 0:
        rates_y, rates_z, x, out, sums, ykeep, zkeep, ytab, ztab, nz, table = refs[:11]
        make_tables(
            dev_y, dev_z, rates_y, rates_z, x.shape[1], x.shape[2], ykeep, zkeep, ytab, ztab, nz, table
        )
    else:
        x, ytab, ztab, nz, _, out, sums = refs[:7]
    band = refs[-1]
    m, n = x.shape[1:]
    pos_z = lax.axis_index("gz")
    r = lax.broadcasted_iota(jnp.int32, (m, n), 0)
    c = lax.broadcasted_iota(jnp.int32, (m, n), 1)
    band[0] = jnp.where(r == c, 1.0, 0.0)
    band[1] = jnp.where((r == c + 1) | (r + 1 == c), 1.0, 0.0)
    z_first = jnp.where(pos_z == 0, 1.0, 0.0).astype(F32)
    z_last = jnp.where(pos_z == dev_z - 1, 1.0, 0.0).astype(F32)
    sub = lax.broadcasted_iota(jnp.int32, (8, n), 0)
    at_head = jnp.where(sub == 0, z_first, 0.0)
    at_tail = jnp.where(sub == 7, z_last, 0.0)

    for k in range(lo, hi):
        g = k - lo

        def rows(ref, i):
            return ref[i, k : k + 1, :]

        phi, chi = columns(rows(ytab, 0), rows(ytab, 1), rows(ytab, 2), m)
        phi_row, chi_row, mid, side = [rows(ytab, i) for i in (3, 4, 5, 6)]
        dmat = jnp.concatenate(
            [
                jnp.minimum(phi[v] * chi_row, chi[v] * phi_row)
                + mid * band[0, 8 * v : 8 * v + 8, :]
                + side * band[1, 8 * v : 8 * v + 8, :]
                for v in range(m // 8)
            ],
            axis=0,
        )
        d_hi, d_lo = split(dmat)
        x_hi, x_lo = split(x[k])
        turned = product(d_hi, d_lo, x_hi, x_lo)
        t_hi, t_lo = split(turned)

        phi, chi = columns(rows(ztab, 0), rows(ztab, 1), rows(ztab, 2), n)
        phi_row, chi_row, mid, side, edge = [rows(ztab, i) for i in (3, 4, 5, 6, 7)]
        head, tail = 1.0 + edge * at_head, 1.0 + edge * at_tail
        phi[0], chi[0] = phi[0] * head, chi[0] * head
        phi[-1], chi[-1] = phi[-1] * tail, chi[-1] * tail
        bmat = jnp.concatenate(
            [
                jnp.minimum(phi[v] * chi_row, chi[v] * phi_row)
                + mid * band[0, 8 * v : 8 * v + 8, :]
                + side * band[1, 8 * v : 8 * v + 8, :]
                for v in range(n // 8)
            ],
            axis=0,
        )
        b_hi, b_lo = split(bmat)
        out[g] = product(t_hi, t_lo, b_hi, b_lo)
        functionals = nz[k]
        f_hi = functionals.astype(BF16).astype(F32)
        f16 = jnp.concatenate([f_hi, functionals - f_hi], axis=0).astype(BF16)
        both = dot(
            jnp.concatenate([f16, f16], axis=1), jnp.concatenate([t_hi, t_lo], axis=1), 1, 1
        )
        sums[g] = both[:8] + both[8:]


def along_lanes(line, f):
    m = line.m
    cell = line.cell
    near = 1.0 - line.power(2 * line.near) * jnp.exp(-2.0 * line.theta * (cell + 1).astype(F32))
    far = 1.0 - line.power(2 * (line.far - m - 1)) * jnp.exp(
        -2.0 * line.theta * (m - cell).astype(F32)
    )
    ups, downs = [], []
    span = 1
    while span < m:
        ratio = line.power(span)
        ups.append((span, jnp.where(cell >= span, ratio, 0.0)))
        downs.append((m - span, jnp.where(cell < m - span, ratio, 0.0)))
        span *= 2
    results = []
    for v in f:
        source = line.weight * v
        up, start = near * source, far * source
        for shift, ratio in ups:
            up = up + ratio * pltpu.roll(up, shift, 1)
        down = start
        for shift, ratio in downs:
            down = down + ratio * pltpu.roll(down, shift, 1)
        down = down - start
        left, right = pltpu.roll(v, 1, 1), pltpu.roll(v, m - 1, 1)
        left = jnp.where(cell > 0, left, 0.0)
        right = jnp.where(cell < m - 1, right, 0.0)
        results.append(far * up + near * down + line.mid * v + line.side * (left + right))
    return results


def place_of(stage):
    position = lax.axis_index("gy")
    size = 1 << stage
    return (position // size) % 2 == 1, position % size, size


def receive(stage, theta, m, held_in, up_sum, down_sum, first, last):
    upper, place, size = place_of(stage)
    steps = jnp.where(upper, place, size - 1 - place).astype(F32)
    scale = jnp.exp(-theta * (m * steps))
    up, down, before, after = held_in
    return (
        jnp.where(upper, up + scale * up_sum, up),
        jnp.where(upper, down, down + scale * down_sum),
        jnp.where(upper & (place == 0), last, before),
        jnp.where(jnp.logical_not(upper) & (place == size - 1), first, after),
    )


def combine_kernel(stage, last_stage, m, mine, got, *refs):
    if stage:
        held_in, ykeep, _, send, held_out = refs
        before = [held_in[i] for i in range(4)]
    else:
        ykeep, _, send, held_out = refs
        before = [jnp.zeros_like(mine[0])] * 4
    theta = ykeep[4]
    upper, _, size = place_of(stage)
    for i, row in enumerate(receive(stage, theta, m, before, got[0], got[1], got[2], got[3])):
        held_out[i] = row
    far = jnp.exp(-theta * (m * size))
    up = jnp.where(upper, mine[0] + far * got[0], got[0] + far * mine[0])
    down = jnp.where(upper, got[1] + far * mine[1], mine[1] + far * got[1])
    first = jnp.where(upper, got[2], mine[2])
    last = jnp.where(upper, mine[3], got[3])
    if stage + 1 < last_stage:
        for i, row in enumerate((up, down, first, last)):
            send[i] = row
    else:
        above, _, _ = place_of(last_stage)
        send[0] = jnp.where(above, down, up)
        send[1] = jnp.where(above, first, last)


def arrivals(stage, m, ykeep, got, held_in):
    before = [held_in[i] for i in range(4)]
    return receive(stage, ykeep[4], m, before, got[0], got[0], got[1], got[1])


def middle_kernel(stage, dev_z, bounds, got, held_in, ykeep, zkeep, *refs):
    pieces, sends, sums = refs[: len(bounds) - 1], refs[len(bounds) - 1 : -1], refs[-1]
    m = ykeep.shape[2]
    pos_z = lax.axis_index("gz")
    n = zkeep.shape[2]
    rows = arrivals(stage, m, ykeep, got, held_in)
    totals = []
    for kind in range(4):
        for piece, lo, hi in zip(pieces, bounds, bounds[1:]):
            sums[kind, lo:hi, :] = piece[:, kind, :]
        total = sums[kind]
        for i, row in enumerate(rows):
            if kind < 2:
                amount = jnp.sum(row * zkeep[5 + kind], axis=1, keepdims=True)
            else:
                amount = row[:, :1] if kind == 2 else row[:, n - 1 :]
            total = total + ykeep[i] * amount
        totals.append(total)
    up, down, head, tail = totals
    for by, send in enumerate(sends):
        ahead = pos_z + by + 1 < dev_z
        send[0] = jnp.where(ahead, up, down)
        send[1] = jnp.where(ahead, tail, head)


def held_kernel(stage, dev_z, rates_z, got, held_in, ykeep, held, table):
    spread(rates_z, table)
    z = Line(table[...], lax.axis_index("gz"), dev_z, table.shape[1])
    z.vectors()
    for i, row in enumerate(along_lanes(z, arrivals(stage, ykeep.shape[2], ykeep, got, held_in))):
        held[i] = row


def final_kernel(dev_z, bounds, held, ykeep, zkeep, *rest):
    gots, rest = rest[: dev_z - 1], rest[dev_z - 1 :]
    local, (out_hbm, out, out_sems, left, right) = rest[:-5], rest[-5:]
    planes, m, n = out.shape
    pos_z = lax.axis_index("gz")
    for i in range(4):
        left[:, i, :] = ykeep[i]
        right[:, i, :] = held[i]
        right[:, 4 + i, :] = zkeep[i]
    reach = zkeep[4]
    up, down = jnp.zeros_like(gots[0][0]), jnp.zeros_like(gots[0][0])
    scale = jnp.ones_like(reach)
    for by in range(dev_z - 1):
        up = up + jnp.where(pos_z > by, scale * gots[by][0], 0.0)
        behind = gots[dev_z - 2 - by]
        down = down + jnp.where(pos_z + by + 1 < dev_z, scale * behind[0], 0.0)
        scale = scale * reach
    left[:, 4, :] = up
    left[:, 5, :] = down
    left[:, 6, :] = jnp.where(pos_z > 0, gots[0][1], 0.0)
    left[:, 7, :] = jnp.where(pos_z < dev_z - 1, gots[-1][1], 0.0)

    count = out_sems.shape[0]
    group = planes // count
    stores = []
    for i in range(count):
        for k in range(i * group, i * group + group):
            a, b = left[k], right[k]
            a_hi, b_hi = a.astype(BF16).astype(F32), b.astype(BF16).astype(F32)
            a_lo, b_lo = a - a_hi, b - b_hi
            a = jnp.concatenate([a_hi, a_lo, a_hi, a_lo], axis=0).astype(BF16)
            b = jnp.concatenate([b_hi, b_hi, b_lo, b_lo], axis=0).astype(BF16)
            piece = sum(k >= hi for hi in bounds[1:])
            out[k] = local[piece][k - bounds[piece]] + dot(a, b, 0, 0)
        some = pl.ds(i * group, group)
        stores.append(pltpu.make_async_copy(out.at[some], out_hbm.at[some], out_sems.at[i]))
        stores[i].start()
    for store in stores:
        store.wait()


def per_device(x, rates_y, rates_z):
    planes, m, n = x.shape
    dev_y, dev_z = lax.axis_size("gy"), lax.axis_size("gz")
    smem = pl.BlockSpec(memory_space=pltpu.SMEM)
    whole = pl.BlockSpec(memory_space=pltpu.VMEM)

    def params():
        return pltpu.CompilerParams(vmem_limit_bytes=VMEM)

    def cost(flops, moved):
        return pl.CostEstimate(flops=flops, bytes_accessed=moved, transcendentals=0)

    def shape(*dims):
        return jax.ShapeDtypeStruct(dims, F32)

    cells = planes * m * n
    hbm = pl.BlockSpec(memory_space=pltpu.HBM)
    hbm = pl.BlockSpec(memory_space=pltpu.HBM)
    send = pl.pallas_call(
        functools.partial(moments_kernel, dev_y),
        in_specs=[hbm, hbm],
        out_specs=whole,
        out_shape=shape(4, planes, n),
        scratch_shapes=[
            pltpu.SMEM((planes,), F32),
            pltpu.VMEM((planes, m, n), F32),
            pltpu.SemaphoreType.DMA,
            pltpu.SemaphoreType.DMA((8,)),
            pltpu.VMEM((planes, n), F32),
            pltpu.VMEM((planes, 8, n), F32),
            pltpu.VMEM((planes, 8, n), F32),
        ],
        compiler_params=pltpu.CompilerParams(vmem_limit_bytes=MOMV * 1024 * 1024),
        cost_estimate=cost(4 * cells, 4 * cells),
        name="moments",
    )(rates_y, x)
    stages = dev_y.bit_length() - 1
    bounds = [planes * i // stages for i in range(stages + 1)]
    parts, pieces = [], []
    held_in = None
    for stage in range(stages):
        lo, hi = bounds[stage], bounds[stage + 1]
        got = lax.ppermute(send, "gy", [(i, i ^ (1 << stage)) for i in range(dev_y)])
        first = stage == 0
        outs = [shape(hi - lo, m, n), shape(hi - lo, 8, m)]
        if first:
            given = (rates_y, rates_z, x)
            in_specs = [smem, smem, whole]
            outs += [
                shape(5, planes, m),
                shape(7, planes, n),
                shape(7, planes, m),
                shape(8, planes, n),
                shape(planes, 8, n),
            ]
            scratch = [pltpu.VMEM((planes, n), F32)]
        else:
            given = (x, *tables, send)
            in_specs = [whole] * 5
            scratch = []
        part, piece, *rest = pl.pallas_call(
            functools.partial(local_kernel, dev_y, dev_z, lo, hi),
            in_specs=in_specs,
            out_specs=[whole] * len(outs),
            out_shape=outs,
            scratch_shapes=scratch
            + [pltpu.VMEM((2, m, n), F32)],
            compiler_params=params(),
            cost_estimate=cost(12 * (hi - lo) * m * m * n, 8 * (hi - lo) * m * n),
            name="local",
        )(*given)
        parts.append(part)
        pieces.append(piece)
        if first:
            ykeep, zkeep, *tables = rest
        if stage + 1 < stages:
            send, held_in = pl.pallas_call(
                functools.partial(combine_kernel, stage, stages - 1, m),
                in_specs=[whole] * (4 if first else 5),
                out_specs=[whole] * 2,
                out_shape=[shape(4 if stage + 2 < stages else 2, planes, n), shape(4, planes, n)],
                compiler_params=params(),
                cost_estimate=cost(planes * n * 20, planes * n * 64),
                name="combine",
            )(send, got, *(() if first else (held_in,)), ykeep, piece)
    sends = pl.pallas_call(
        functools.partial(middle_kernel, stages - 1, dev_z, bounds),
        in_specs=[whole] * (4 + stages),
        out_specs=[whole] * (dev_z - 1),
        out_shape=[shape(2, planes, m)] * (dev_z - 1),
        scratch_shapes=[pltpu.VMEM((4, planes, m), F32)],
        compiler_params=params(),
        cost_estimate=cost(planes * n * 100, planes * n * 100),
        name="middle",
    )(got, held_in, ykeep, zkeep, *pieces)
    got_z = [
        lax.ppermute(send, "gz", [(i, (i + by + 1) % dev_z) for i in range(dev_z)])
        for by, send in enumerate(sends)
    ]
    held = pl.pallas_call(
        functools.partial(held_kernel, stages - 1, dev_z),
        in_specs=[smem, whole, whole, whole],
        out_specs=whole,
        out_shape=shape(4, planes, n),
        scratch_shapes=[pltpu.VMEM((planes, n), F32)],
        compiler_params=params(),
        cost_estimate=cost(planes * n * 400, planes * n * 100),
        name="held",
    )(rates_z, got, held_in, ykeep)
    return pl.pallas_call(
        functools.partial(final_kernel, dev_z, bounds),
        in_specs=[whole] * (dev_z + 2 + stages),
        out_specs=hbm,
        out_shape=shape(planes, m, n),
        scratch_shapes=[
            pltpu.VMEM((planes, m, n), F32),
            pltpu.SemaphoreType.DMA((4,)),
            pltpu.VMEM((planes, 8, m), F32),
            pltpu.VMEM((planes, 8, n), F32),
        ],
        compiler_params=params(),
        cost_estimate=cost(64 * cells, 8 * cells),
        name="final",
    )(held, ykeep, zkeep, *got_z, *parts)


def solution(mesh):
    return jax.shard_map(
        per_device,
        mesh=mesh,
        in_specs=(P(None, "gy", "gz"), P(), P()),
        out_specs=P(None, "gy", "gz"),
        check_vma=False,
    )
```

```python
import functools

import jax
import jax.numpy as jnp
from jax import lax
from jax.experimental import pallas as pl
from jax.experimental.pallas import tpu as pltpu
from jax.sharding import PartitionSpec as P

alpha = 2.0 / 11.0
inner_weight = 12.0 / 11.0
outer_weight = 3.0 / 44.0
F32 = jnp.float32
BF16 = jnp.bfloat16
VMEM = 24 * 1024 * 1024
FETCH_VMEM = 50 * 1024 * 1024
CUTS = (0, 2, 5, 10, 16)


def spread(rates, table):
    for k in range(table.shape[0]):
        table[pl.ds(k, 1), :] = jnp.full((1, table.shape[1]), rates[k], F32)


class Line:
    def __init__(self, rate, position, devices, m):
        beside = inner_weight * rate - alpha
        eps = (1.0 + 2.0 * alpha) / (2.0 * beside)
        sinh = jnp.sqrt(eps * (2.0 + eps))
        corner = rate * outer_weight
        self.m = m
        self.theta = jnp.log1p(eps + sinh)
        total = m * devices
        self.far = total + 1 - m * position
        self.near = m * position
        self.c = m // 2
        self.green = 1.0 / (2.0 * beside * sinh * (1.0 - self.power(2 * (total + 1))))
        self.rho = 1.0 + 2.0 * alpha * (1.0 + eps) + 4.0 * corner * eps * (2.0 + eps)
        self.side = -corner / beside
        self.mid = 2.0 * self.side * (1.0 + eps) - alpha / beside
        self.corner = corner
        self.is_first = jnp.where(position == 0, 1.0, 0.0).astype(F32)
        self.is_last = jnp.where(position == devices - 1, 1.0, 0.0).astype(F32)
        self.cell = lax.broadcasted_iota(jnp.int32, rate.shape, 1)

    def power(self, n):
        return jnp.exp(-self.theta * jnp.asarray(n, F32))

    def vectors(self):
        i = (self.cell + (1 - self.c)).astype(F32)
        down, up = jnp.exp(-self.theta * i), jnp.exp(self.theta * i)
        self.cut_far = self.power(2 * (self.far - self.c))
        self.cut_near = self.power(2 * (self.near + self.c))
        self.phi = down - self.cut_far * up
        self.chi = up - self.cut_near * down
        self.ends = jnp.where(self.cell == 0, self.is_first, 0.0) + jnp.where(
            self.cell == self.m - 1, self.is_last, 0.0
        )
        self.weight = self.green * (self.rho + self.corner * self.ends)
        self.send_up = self.weight * self.chi * self.power(self.m - self.c)
        self.send_down = self.weight * self.phi * self.power(self.c - 1)
        self.get_up = self.phi * self.power(self.c)
        self.get_down = self.chi * self.power(self.m + 1 - self.c)
        self.head = jnp.where(self.cell == 0, 1.0, 0.0).astype(F32)
        self.tail = jnp.where(self.cell == self.m - 1, 1.0, 0.0).astype(F32)


def split(a):
    hi = a.astype(BF16)
    return hi, (a - hi.astype(F32)).astype(BF16)


def dot(a, b, ca, cb):
    return lax.dot_general(a, b, (((ca,), (cb,)), ((), ())), preferred_element_type=F32)


def product(a_hi, a_lo, b_hi, b_lo):
    b = jnp.concatenate([b_hi, b_lo], axis=1)
    n = b_hi.shape[1]
    both = dot(jnp.concatenate([a_hi, a_lo], axis=1), jnp.concatenate([b, b], axis=0), 1, 0)
    return both[:, :n] + both[:, n:]


def fetch_kernel(x_hbm, x, sems):
    parts = sems.shape[0]
    group = x.shape[0] // parts
    copies = []
    for i in range(parts):
        some = pl.ds(i * group, group)
        copies.append(pltpu.make_async_copy(x_hbm.at[some], x.at[some], sems.at[i]))
        copies[i].start()
    for copy in copies:
        copy.wait()


def moments_kernel(devices, rates, x, out, table, up_rows, down_rows):
    planes, m, n = x.shape
    position = lax.axis_index("gy")
    spread(rates, table)
    line = Line(table[...], position, devices, m)
    one = line.power(1)
    eighth = line.power(8)
    across = line.power(m - 1)
    lower_scale, upper_scale = line.corner * line.is_first, line.corner * line.is_last
    turn_up, turn_down = line.power(2 * line.near + m + 1), line.power(2 * line.far - m - 1)
    table[...] = eighth
    if True:
        for k in range(planes):
            ratio = jnp.broadcast_to(table[k : k + 1, :], (8, n))
            up, down = x[k, 0:8, :], x[k, m - 8 : m, :]
            for v in range(1, m // 8):
                up = up * ratio + x[k, 8 * v : 8 * v + 8, :]
                w = m - 8 - 8 * v
                down = down * ratio + x[k, w : w + 8, :]
            up_rows[k] = up
            down_rows[k] = down
    up, down = up_rows[:, 0, :], down_rows[:, 7, :]
    for s in range(1, 8):
        up = up * one + up_rows[:, s, :]
        down = down * one + down_rows[:, 7 - s, :]
    first, last = x[:, 0, :], x[:, m - 1, :]
    lower, upper = lower_scale * first, upper_scale * last
    up = line.rho * up + across * lower + upper
    down = line.rho * down + lower + across * upper
    going_up = line.green * (up - turn_up * down)
    going_down = line.green * (down - turn_down * up)
    out[0] = going_up
    out[1] = going_down
    out[2] = first
    out[3] = last


def columns(theta, cut_far, cut_near, m):
    shape = (8, theta.shape[1])
    i = (lax.broadcasted_iota(jnp.int32, shape, 0) + (1 - m // 2)).astype(F32)
    down, up = jnp.exp(-theta * i), jnp.exp(theta * i)
    grow, fall = jnp.exp(theta * 8.0), jnp.exp(theta * -8.0)
    phi, chi = [], []
    for _ in range(m // 8):
        phi.append(down - cut_far * up)
        chi.append(up - cut_near * down)
        down, up = down * fall, up * grow
    return phi, chi


def make_tables(dev_y, dev_z, rates_y, rates_z, m, n, ykeep, zkeep, ytab, ztab, nz, table):
    pos_y, pos_z = lax.axis_index("gy"), lax.axis_index("gz")
    spread(rates_y, table)
    y = Line(table[...], pos_y, dev_y, m)
    y.vectors()
    for i, row in enumerate((y.get_up, y.get_down, y.side * y.head, y.side * y.tail, y.theta)):
        ykeep[i] = row
    for i, row in enumerate(
        (y.theta, y.cut_far, y.cut_near, y.phi * y.weight, y.chi * y.weight, y.mid, y.side)
    ):
        ytab[i] = row
    spread(rates_z, table)
    z = Line(table[...], pos_z, dev_z, n)
    z.vectors()
    for i, row in enumerate(
        (z.get_up, z.get_down, z.side * z.head, z.side * z.tail, z.power(n), z.send_up, z.send_down)
    ):
        zkeep[i] = row
    base = z.green * z.rho
    for i, row in enumerate(
        (z.theta, z.cut_far, z.cut_near, z.phi * base, z.chi * base, z.mid, z.side, z.corner / z.rho)
    ):
        ztab[i] = row
    for i, row in enumerate((z.send_up, z.send_down, z.head, z.tail)):
        nz[:, i, :] = row
        nz[:, 4 + i, :] = jnp.zeros_like(row)


def local_kernel(dev_y, dev_z, lo, hi, *refs):
    if lo == 0:
        rates_y, rates_z, x, out, sums, ykeep, zkeep, ytab, ztab, nz, table = refs[:11]
        make_tables(
            dev_y, dev_z, rates_y, rates_z, x.shape[1], x.shape[2], ykeep, zkeep, ytab, ztab, nz, table
        )
    else:
        x, ytab, ztab, nz, _, out, sums = refs[:7]
    band = refs[-1]
    m, n = x.shape[1:]
    pos_z = lax.axis_index("gz")
    r = lax.broadcasted_iota(jnp.int32, (m, n), 0)
    c = lax.broadcasted_iota(jnp.int32, (m, n), 1)
    band[0] = jnp.where(r == c, 1.0, 0.0)
    band[1] = jnp.where((r == c + 1) | (r + 1 == c), 1.0, 0.0)
    z_first = jnp.where(pos_z == 0, 1.0, 0.0).astype(F32)
    z_last = jnp.where(pos_z == dev_z - 1, 1.0, 0.0).astype(F32)
    sub = lax.broadcasted_iota(jnp.int32, (8, n), 0)
    at_head = jnp.where(sub == 0, z_first, 0.0)
    at_tail = jnp.where(sub == 7, z_last, 0.0)

    for k in range(lo, hi):
        g = k - lo

        def rows(ref, i):
            return ref[i, k : k + 1, :]

        phi, chi = columns(rows(ytab, 0), rows(ytab, 1), rows(ytab, 2), m)
        phi_row, chi_row, mid, side = [rows(ytab, i) for i in (3, 4, 5, 6)]
        dmat = jnp.concatenate(
            [
                jnp.minimum(phi[v] * chi_row, chi[v] * phi_row)
                + mid * band[0, 8 * v : 8 * v + 8, :]
                + side * band[1, 8 * v : 8 * v + 8, :]
                for v in range(m // 8)
            ],
            axis=0,
        )
        d_hi, d_lo = split(dmat)
        x_hi, x_lo = split(x[k])
        turned = product(d_hi, d_lo, x_hi, x_lo)
        t_hi, t_lo = split(turned)

        phi, chi = columns(rows(ztab, 0), rows(ztab, 1), rows(ztab, 2), n)
        phi_row, chi_row, mid, side, edge = [rows(ztab, i) for i in (3, 4, 5, 6, 7)]
        head, tail = 1.0 + edge * at_head, 1.0 + edge * at_tail
        phi[0], chi[0] = phi[0] * head, chi[0] * head
        phi[-1], chi[-1] = phi[-1] * tail, chi[-1] * tail
        bmat = jnp.concatenate(
            [
                jnp.minimum(phi[v] * chi_row, chi[v] * phi_row)
                + mid * band[0, 8 * v : 8 * v + 8, :]
                + side * band[1, 8 * v : 8 * v + 8, :]
                for v in range(n // 8)
            ],
            axis=0,
        )
        b_hi, b_lo = split(bmat)
        out[g] = product(t_hi, t_lo, b_hi, b_lo)
        functionals = nz[k]
        f_hi = functionals.astype(BF16).astype(F32)
        f16 = jnp.concatenate([f_hi, functionals - f_hi], axis=0).astype(BF16)
        both = dot(
            jnp.concatenate([f16, f16], axis=1), jnp.concatenate([t_hi, t_lo], axis=1), 1, 1
        )
        sums[g] = both[:8] + both[8:]


def along_lanes(line, f):
    m = line.m
    cell = line.cell
    near = 1.0 - line.power(2 * line.near) * jnp.exp(-2.0 * line.theta * (cell + 1).astype(F32))
    far = 1.0 - line.power(2 * (line.far - m - 1)) * jnp.exp(
        -2.0 * line.theta * (m - cell).astype(F32)
    )
    ups, downs = [], []
    span = 1
    while span < m:
        ratio = line.power(span)
        ups.append((span, jnp.where(cell >= span, ratio, 0.0)))
        downs.append((m - span, jnp.where(cell < m - span, ratio, 0.0)))
        span *= 2
    results = []
    for v in f:
        source = line.weight * v
        up, start = near * source, far * source
        for shift, ratio in ups:
            up = up + ratio * pltpu.roll(up, shift, 1)
        down = start
        for shift, ratio in downs:
            down = down + ratio * pltpu.roll(down, shift, 1)
        down = down - start
        left, right = pltpu.roll(v, 1, 1), pltpu.roll(v, m - 1, 1)
        left = jnp.where(cell > 0, left, 0.0)
        right = jnp.where(cell < m - 1, right, 0.0)
        results.append(far * up + near * down + line.mid * v + line.side * (left + right))
    return results


def place_of(stage):
    position = lax.axis_index("gy")
    size = 1 << stage
    return (position // size) % 2 == 1, position % size, size


def receive(stage, theta, m, held_in, up_sum, down_sum, first, last):
    upper, place, size = place_of(stage)
    steps = jnp.where(upper, place, size - 1 - place).astype(F32)
    scale = jnp.exp(-theta * (m * steps))
    up, down, before, after = held_in
    return (
        jnp.where(upper, up + scale * up_sum, up),
        jnp.where(upper, down, down + scale * down_sum),
        jnp.where(upper & (place == 0), last, before),
        jnp.where(jnp.logical_not(upper) & (place == size - 1), first, after),
    )


def combine_kernel(stage, last_stage, m, mine, got, *refs):
    if stage:
        held_in, ykeep, _, send, held_out = refs
        before = [held_in[i] for i in range(4)]
    else:
        ykeep, _, send, held_out = refs
        before = [jnp.zeros_like(mine[0])] * 4
    theta = ykeep[4]
    upper, _, size = place_of(stage)
    row, end = got.shape[0] - 1, got.shape[0] - 2 if stage == 0 else got.shape[0] - 1
    lows = (got[0], got[1], got[end], got[row])
    for i, value in enumerate(receive(stage, theta, m, before, *lows)):
        held_out[i] = value
    far = jnp.exp(-theta * (m * size))
    up = jnp.where(upper, mine[0] + far * got[0], got[0] + far * mine[0])
    down = jnp.where(upper, got[1] + far * mine[1], mine[1] + far * got[1])
    _, place, _ = place_of(stage + 1)
    if stage == 0:
        first = jnp.where(upper, got[2], mine[2])
        last = jnp.where(upper, mine[3], got[3])
        halo = jnp.where(place == 0, last, first)
    else:
        halo = got[2]
    if stage + 1 < last_stage:
        send[0] = up
        send[1] = down
        send[2] = halo
    else:
        above, _, _ = place_of(last_stage)
        send[0] = jnp.where(above, down, up)
        send[1] = halo


def arrivals(stage, m, ykeep, got, held_in):
    before = [held_in[i] for i in range(4)]
    return receive(stage, ykeep[4], m, before, got[0], got[0], got[1], got[1])


def middle_kernel(stage, dev_z, bounds, got, held_in, ykeep, zkeep, *refs):
    pieces, sends, sums = refs[: len(bounds) - 1], refs[len(bounds) - 1 : -1], refs[-1]
    m = ykeep.shape[2]
    pos_z = lax.axis_index("gz")
    n = zkeep.shape[2]
    rows = arrivals(stage, m, ykeep, got, held_in)
    totals = []
    for kind in range(4):
        for piece, lo, hi in zip(pieces, bounds, bounds[1:]):
            sums[kind, lo:hi, :] = piece[:, kind, :]
        total = sums[kind]
        for i, row in enumerate(rows):
            if kind < 2:
                amount = jnp.sum(row * zkeep[5 + kind], axis=1, keepdims=True)
            else:
                amount = row[:, :1] if kind == 2 else row[:, n - 1 :]
            total = total + ykeep[i] * amount
        totals.append(total)
    up, down, head, tail = totals
    for by, send in enumerate(sends):
        ahead = pos_z + by + 1 < dev_z
        send[0] = jnp.where(ahead, up, down)
        send[1] = jnp.where(ahead, tail, head)


def held_kernel(stage, dev_z, rates_z, got, held_in, ykeep, zkeep, right_split, table, right):
    spread(rates_z, table)
    z = Line(table[...], lax.axis_index("gz"), dev_z, table.shape[1])
    z.vectors()
    for i, row in enumerate(along_lanes(z, arrivals(stage, ykeep.shape[2], ykeep, got, held_in))):
        right[:, i, :] = row
        right[:, 4 + i, :] = zkeep[i]
    b = right[...]
    hi = b.astype(BF16).astype(F32)
    lo = b - hi
    right_split[...] = jnp.concatenate([hi, hi, lo, lo], axis=1).astype(BF16)


def final_kernel(dev_z, bounds, right, ykeep, zkeep, *rest):
    gots, rest = rest[: dev_z - 1], rest[dev_z - 1 :]
    local, (out_hbm, out, out_sems, left) = rest[:-4], rest[-4:]
    planes, m, n = out.shape
    pos_z = lax.axis_index("gz")
    for i in range(4):
        left[:, i, :] = ykeep[i]
    reach = zkeep[4]
    up, down = jnp.zeros_like(gots[0][0]), jnp.zeros_like(gots[0][0])
    scale = jnp.ones_like(reach)
    for by in range(dev_z - 1):
        up = up + jnp.where(pos_z > by, scale * gots[by][0], 0.0)
        behind = gots[dev_z - 2 - by]
        down = down + jnp.where(pos_z + by + 1 < dev_z, scale * behind[0], 0.0)
        scale = scale * reach
    left[:, 4, :] = up
    left[:, 5, :] = down
    left[:, 6, :] = jnp.where(pos_z > 0, gots[0][1], 0.0)
    left[:, 7, :] = jnp.where(pos_z < dev_z - 1, gots[-1][1], 0.0)

    cuts = [planes * c // 16 for c in CUTS]
    stores = []
    for i, (lo, hi) in enumerate(zip(cuts, cuts[1:])):
        for k in range(lo, hi):
            a = left[k]
            a_hi = a.astype(BF16).astype(F32)
            a_lo = a - a_hi
            a = jnp.concatenate([a_hi, a_lo, a_hi, a_lo], axis=0).astype(BF16)
            piece = sum(k >= bound for bound in bounds[1:])
            out[k] = local[piece][k - bounds[piece]] + dot(a, right[k], 0, 0)
        some = pl.ds(lo, hi - lo)
        stores.append(pltpu.make_async_copy(out.at[some], out_hbm.at[some], out_sems.at[i]))
        stores[i].start()
    for store in stores:
        store.wait()


def per_device(x, rates_y, rates_z):
    planes, m, n = x.shape
    dev_y, dev_z = lax.axis_size("gy"), lax.axis_size("gz")
    smem = pl.BlockSpec(memory_space=pltpu.SMEM)
    whole = pl.BlockSpec(memory_space=pltpu.VMEM)

    def params():
        return pltpu.CompilerParams(vmem_limit_bytes=VMEM)

    def cost(flops, moved):
        return pl.CostEstimate(flops=flops, bytes_accessed=moved, transcendentals=0)

    def shape(*dims):
        return jax.ShapeDtypeStruct(dims, F32)

    cells = planes * m * n
    hbm = pl.BlockSpec(memory_space=pltpu.HBM)
    hbm = pl.BlockSpec(memory_space=pltpu.HBM)
    x = pl.pallas_call(
        fetch_kernel,
        in_specs=[hbm],
        out_specs=whole,
        out_shape=shape(planes, m, n),
        scratch_shapes=[pltpu.SemaphoreType.DMA((8,))],
        compiler_params=pltpu.CompilerParams(vmem_limit_bytes=FETCH_VMEM),
        cost_estimate=cost(4, 8 * cells),
        name="fetch",
    )(x)
    send = pl.pallas_call(
        functools.partial(moments_kernel, dev_y),
        in_specs=[smem, whole],
        out_specs=whole,
        out_shape=shape(4, planes, n),
        scratch_shapes=[
            pltpu.VMEM((planes, n), F32),
            pltpu.VMEM((planes, 8, n), F32),
            pltpu.VMEM((planes, 8, n), F32),
        ],
        compiler_params=params(),
        cost_estimate=cost(4 * cells, 4 * cells),
        name="moments",
    )(rates_y, x)
    stages = dev_y.bit_length() - 1
    bounds = [planes * i // stages for i in range(stages + 1)]
    parts, pieces = [], []
    held_in = None
    for stage in range(stages):
        lo, hi = bounds[stage], bounds[stage + 1]
        got = lax.ppermute(send, "gy", [(i, i ^ (1 << stage)) for i in range(dev_y)])
        first = stage == 0
        outs = [shape(hi - lo, m, n), shape(hi - lo, 8, m)]
        if first:
            given = (rates_y, rates_z, x)
            in_specs = [smem, smem, whole]
            outs += [
                shape(5, planes, m),
                shape(7, planes, n),
                shape(7, planes, m),
                shape(8, planes, n),
                shape(planes, 8, n),
            ]
            scratch = [pltpu.VMEM((planes, n), F32)]
        else:
            given = (x, *tables, send)
            in_specs = [whole] * 5
            scratch = []
        part, piece, *rest = pl.pallas_call(
            functools.partial(local_kernel, dev_y, dev_z, lo, hi),
            in_specs=in_specs,
            out_specs=[whole] * len(outs),
            out_shape=outs,
            scratch_shapes=scratch
            + [pltpu.VMEM((2, m, n), F32)],
            compiler_params=params(),
            cost_estimate=cost(12 * (hi - lo) * m * m * n, 8 * (hi - lo) * m * n),
            name="local",
        )(*given)
        parts.append(part)
        pieces.append(piece)
        if first:
            ykeep, zkeep, *tables = rest
        if stage + 1 < stages:
            send, held_in = pl.pallas_call(
                functools.partial(combine_kernel, stage, stages - 1, m),
                in_specs=[whole] * (4 if first else 5),
                out_specs=[whole] * 2,
                out_shape=[shape(3 if stage + 2 < stages else 2, planes, n), shape(4, planes, n)],
                compiler_params=params(),
                cost_estimate=cost(planes * n * 20, planes * n * 64),
                name="combine",
            )(send, got, *(() if first else (held_in,)), ykeep, piece)
    sends = pl.pallas_call(
        functools.partial(middle_kernel, stages - 1, dev_z, bounds),
        in_specs=[whole] * (4 + stages),
        out_specs=[whole] * (dev_z - 1),
        out_shape=[shape(2, planes, m)] * (dev_z - 1),
        scratch_shapes=[pltpu.VMEM((4, planes, m), F32)],
        compiler_params=params(),
        cost_estimate=cost(planes * n * 100, planes * n * 100),
        name="middle",
    )(got, held_in, ykeep, zkeep, *pieces)
    got_z = [
        lax.ppermute(send, "gz", [(i, (i + by + 1) % dev_z) for i in range(dev_z)])
        for by, send in enumerate(sends)
    ]
    held = pl.pallas_call(
        functools.partial(held_kernel, stages - 1, dev_z),
        in_specs=[smem, whole, whole, whole, whole],
        out_specs=whole,
        out_shape=jax.ShapeDtypeStruct((planes, 32, n), BF16),
        scratch_shapes=[pltpu.VMEM((planes, n), F32), pltpu.VMEM((planes, 8, n), F32)],
        compiler_params=params(),
        cost_estimate=cost(planes * n * 400, planes * n * 100),
        name="held",
    )(rates_z, got, held_in, ykeep, zkeep)
    return pl.pallas_call(
        functools.partial(final_kernel, dev_z, bounds),
        in_specs=[whole] * (dev_z + 2 + stages),
        out_specs=hbm,
        out_shape=shape(planes, m, n),
        scratch_shapes=[
            pltpu.VMEM((planes, m, n), F32),
            pltpu.SemaphoreType.DMA((len(CUTS) - 1,)),
            pltpu.VMEM((planes, 8, m), F32),
        ],
        compiler_params=params(),
        cost_estimate=cost(64 * cells, 8 * cells),
        name="final",
    )(held, ykeep, zkeep, *got_z, *parts)


def solution(mesh):
    return jax.shard_map(
        per_device,
        mesh=mesh,
        in_specs=(P(None, "gy", "gz"), P(), P()),
        out_specs=P(None, "gy", "gz"),
        check_vma=False,
    )
```

```python
import functools

import jax
import jax.numpy as jnp
from jax import lax
from jax.experimental import pallas as pl
from jax.experimental.pallas import tpu as pltpu
from jax.sharding import PartitionSpec as P

alpha = 2.0 / 11.0
inner_weight = 12.0 / 11.0
outer_weight = 3.0 / 44.0
F32 = jnp.float32
BF16 = jnp.bfloat16
VMEM = 24 * 1024 * 1024
FETCH_VMEM = 50 * 1024 * 1024
CUTS = (0, 2, 5, 10, 16)


def down_sublanes(rates, lanes):
    planes = rates.shape[0]
    row = jnp.broadcast_to(rates[...].reshape(1, planes), (planes, planes))
    diagonal = lax.broadcasted_iota(jnp.int32, row.shape, 0) == lax.broadcasted_iota(
        jnp.int32, row.shape, 1
    )
    column = jnp.sum(jnp.where(diagonal, row, 0.0), axis=1, keepdims=True)
    return jnp.broadcast_to(column, (planes, lanes))


class Line:
    def __init__(self, rate, position, devices, m):
        beside = inner_weight * rate - alpha
        eps = (1.0 + 2.0 * alpha) / (2.0 * beside)
        sinh = jnp.sqrt(eps * (2.0 + eps))
        corner = rate * outer_weight
        self.m = m
        self.growth = 1.0 + (eps + sinh)
        self.theta = jnp.log1p(eps + sinh)
        total = m * devices
        self.far = total + 1 - m * position
        self.near = m * position
        self.c = m // 2
        self.green = 1.0 / (2.0 * beside * sinh * (1.0 - self.power(2 * (total + 1))))
        self.rho = 1.0 + 2.0 * alpha * (1.0 + eps) + 4.0 * corner * eps * (2.0 + eps)
        self.side = -corner / beside
        self.mid = 2.0 * self.side * (1.0 + eps) - alpha / beside
        self.corner = corner
        self.is_first = jnp.where(position == 0, 1.0, 0.0).astype(F32)
        self.is_last = jnp.where(position == devices - 1, 1.0, 0.0).astype(F32)
        self.cell = lax.broadcasted_iota(jnp.int32, rate.shape, 1)

    def power(self, n):
        return jnp.exp(-self.theta * jnp.asarray(n, F32))

    def vectors(self):
        i = (self.cell + (1 - self.c)).astype(F32)
        down, up = jnp.exp(-self.theta * i), jnp.exp(self.theta * i)
        self.cut_far = self.power(2 * (self.far - self.c))
        self.cut_near = self.power(2 * (self.near + self.c))
        self.phi = down - self.cut_far * up
        self.chi = up - self.cut_near * down
        self.ends = jnp.where(self.cell == 0, self.is_first, 0.0) + jnp.where(
            self.cell == self.m - 1, self.is_last, 0.0
        )
        self.weight = self.green * (self.rho + self.corner * self.ends)
        self.send_up = self.weight * self.chi * self.power(self.m - self.c)
        self.send_down = self.weight * self.phi * self.power(self.c - 1)
        self.get_up = self.phi * self.power(self.c)
        self.get_down = self.chi * self.power(self.m + 1 - self.c)
        self.head = jnp.where(self.cell == 0, 1.0, 0.0).astype(F32)
        self.tail = jnp.where(self.cell == self.m - 1, 1.0, 0.0).astype(F32)


def split(a):
    hi = a.astype(BF16)
    return hi, (a - hi.astype(F32)).astype(BF16)


def dot(a, b, ca, cb):
    return lax.dot_general(a, b, (((ca,), (cb,)), ((), ())), preferred_element_type=F32)


def product(a_hi, a_lo, b_hi, b_lo):
    b = jnp.concatenate([b_hi, b_lo], axis=1)
    n = b_hi.shape[1]
    both = dot(jnp.concatenate([a_hi, a_lo], axis=1), jnp.concatenate([b, b], axis=0), 1, 0)
    return both[:, :n] + both[:, n:]


def fetch_kernel(x_hbm, x, sems):
    parts = sems.shape[0]
    group = x.shape[0] // parts
    copies = []
    for i in range(parts):
        some = pl.ds(i * group, group)
        copies.append(pltpu.make_async_copy(x_hbm.at[some], x.at[some], sems.at[i]))
        copies[i].start()
    for copy in copies:
        copy.wait()


def moments_kernel(devices, rates, x, out, table, up_rows, down_rows):
    planes, m, n = x.shape
    position = lax.axis_index("gy")
    line = Line(down_sublanes(rates, n), position, devices, m)
    one = 1.0 / line.growth
    eighth = one * one
    eighth = eighth * eighth
    eighth = eighth * eighth
    across = line.power(m - 1)
    lower_scale, upper_scale = line.corner * line.is_first, line.corner * line.is_last
    turn_up, turn_down = line.power(2 * line.near + m + 1), line.power(2 * line.far - m - 1)
    table[...] = eighth
    for k in range(planes):
        ratio = jnp.broadcast_to(table[k : k + 1, :], (8, n))
        rows = [x[k, v : v + 8, :] for v in range(0, m, 8)]
        up, down = rows[0], rows[-1]
        for ahead, behind in zip(rows[1:], rows[-2::-1]):
            up = up * ratio + ahead
            down = down * ratio + behind
        up_rows[k] = up
        down_rows[k] = down
    up, down = up_rows[:, 0, :], down_rows[:, 7, :]
    for s in range(1, 8):
        up = up * one + up_rows[:, s, :]
        down = down * one + down_rows[:, 7 - s, :]
    first, last = x[:, 0, :], x[:, m - 1, :]
    lower, upper = lower_scale * first, upper_scale * last
    up = line.rho * up + across * lower + upper
    down = line.rho * down + lower + across * upper
    going_up = line.green * (up - turn_up * down)
    going_down = line.green * (down - turn_down * up)
    out[0] = going_up
    out[1] = going_down
    out[2] = first
    out[3] = last


def columns(theta, cut_far, cut_near, m):
    shape = (8, theta.shape[1])
    i = (lax.broadcasted_iota(jnp.int32, shape, 0) + (1 - m // 2)).astype(F32)
    down, up = jnp.exp(-theta * i), jnp.exp(theta * i)
    grow, fall = jnp.exp(theta * 8.0), jnp.exp(theta * -8.0)
    phi, chi = [], []
    for _ in range(m // 8):
        phi.append(down - cut_far * up)
        chi.append(up - cut_near * down)
        down, up = down * fall, up * grow
    return phi, chi


def make_tables(dev_y, dev_z, rates_y, rates_z, m, n, ykeep, zkeep, ytab, ztab, nz):
    pos_y, pos_z = lax.axis_index("gy"), lax.axis_index("gz")
    y = Line(down_sublanes(rates_y, m), pos_y, dev_y, m)
    y.vectors()
    for i, row in enumerate((y.get_up, y.get_down, y.side * y.head, y.side * y.tail, y.theta)):
        ykeep[i] = row
    for i, row in enumerate(
        (y.theta, y.cut_far, y.cut_near, y.phi * y.weight, y.chi * y.weight, y.mid, y.side)
    ):
        ytab[i] = row
    z = Line(down_sublanes(rates_z, n), pos_z, dev_z, n)
    z.vectors()
    for i, row in enumerate(
        (z.get_up, z.get_down, z.side * z.head, z.side * z.tail, z.power(n), z.send_up, z.send_down)
    ):
        zkeep[i] = row
    base = z.green * z.rho
    for i, row in enumerate(
        (z.theta, z.cut_far, z.cut_near, z.phi * base, z.chi * base, z.mid, z.side, z.corner / z.rho)
    ):
        ztab[i] = row
    for i, row in enumerate((z.send_up, z.send_down, z.head, z.tail)):
        nz[:, i, :] = row
        nz[:, 4 + i, :] = jnp.zeros_like(row)


def local_kernel(dev_y, dev_z, lo, hi, *refs):
    if lo == 0:
        rates_y, rates_z, x, out, sums, ykeep, zkeep, ytab, ztab, nz = refs[:10]
        make_tables(
            dev_y, dev_z, rates_y, rates_z, x.shape[1], x.shape[2], ykeep, zkeep, ytab, ztab, nz
        )
    else:
        x, ytab, ztab, nz, _, out, sums = refs[:7]
    band = refs[-1]
    m, n = x.shape[1:]
    pos_z = lax.axis_index("gz")
    r = lax.broadcasted_iota(jnp.int32, (m, n), 0)
    c = lax.broadcasted_iota(jnp.int32, (m, n), 1)
    band[0] = jnp.where(r == c, 1.0, 0.0)
    band[1] = jnp.where((r == c + 1) | (r + 1 == c), 1.0, 0.0)
    z_first = jnp.where(pos_z == 0, 1.0, 0.0).astype(F32)
    z_last = jnp.where(pos_z == dev_z - 1, 1.0, 0.0).astype(F32)
    sub = lax.broadcasted_iota(jnp.int32, (8, n), 0)
    at_head = jnp.where(sub == 0, z_first, 0.0)
    at_tail = jnp.where(sub == 7, z_last, 0.0)

    for k in range(lo, hi):
        g = k - lo

        def rows(ref, i):
            return ref[i, k : k + 1, :]

        phi, chi = columns(rows(ytab, 0), rows(ytab, 1), rows(ytab, 2), m)
        phi_row, chi_row, mid, side = [rows(ytab, i) for i in (3, 4, 5, 6)]
        dmat = jnp.concatenate(
            [
                jnp.minimum(phi[v] * chi_row, chi[v] * phi_row)
                + mid * band[0, 8 * v : 8 * v + 8, :]
                + side * band[1, 8 * v : 8 * v + 8, :]
                for v in range(m // 8)
            ],
            axis=0,
        )
        d_hi, d_lo = split(dmat)
        x_hi, x_lo = split(x[k])
        turned = product(d_hi, d_lo, x_hi, x_lo)
        t_hi, t_lo = split(turned)

        phi, chi = columns(rows(ztab, 0), rows(ztab, 1), rows(ztab, 2), n)
        phi_row, chi_row, mid, side, edge = [rows(ztab, i) for i in (3, 4, 5, 6, 7)]
        head, tail = 1.0 + edge * at_head, 1.0 + edge * at_tail
        phi[0], chi[0] = phi[0] * head, chi[0] * head
        phi[-1], chi[-1] = phi[-1] * tail, chi[-1] * tail
        bmat = jnp.concatenate(
            [
                jnp.minimum(phi[v] * chi_row, chi[v] * phi_row)
                + mid * band[0, 8 * v : 8 * v + 8, :]
                + side * band[1, 8 * v : 8 * v + 8, :]
                for v in range(n // 8)
            ],
            axis=0,
        )
        b_hi, b_lo = split(bmat)
        out[g] = product(t_hi, t_lo, b_hi, b_lo)
        functionals = nz[k]
        f_hi = functionals.astype(BF16).astype(F32)
        f16 = jnp.concatenate([f_hi, functionals - f_hi], axis=0).astype(BF16)
        both = dot(
            jnp.concatenate([f16, f16], axis=1), jnp.concatenate([t_hi, t_lo], axis=1), 1, 1
        )
        sums[g] = both[:8] + both[8:]


def along_lanes(line, f):
    m = line.m
    cell = line.cell
    near = 1.0 - line.power(2 * line.near) * jnp.exp(-2.0 * line.theta * (cell + 1).astype(F32))
    far = 1.0 - line.power(2 * (line.far - m - 1)) * jnp.exp(
        -2.0 * line.theta * (m - cell).astype(F32)
    )
    ups, downs = [], []
    span = 1
    while span < m:
        ratio = line.power(span)
        ups.append((span, jnp.where(cell >= span, ratio, 0.0)))
        downs.append((m - span, jnp.where(cell < m - span, ratio, 0.0)))
        span *= 2
    results = []
    for v in f:
        source = line.weight * v
        up, start = near * source, far * source
        for shift, ratio in ups:
            up = up + ratio * pltpu.roll(up, shift, 1)
        down = start
        for shift, ratio in downs:
            down = down + ratio * pltpu.roll(down, shift, 1)
        down = down - start
        left, right = pltpu.roll(v, 1, 1), pltpu.roll(v, m - 1, 1)
        left = jnp.where(cell > 0, left, 0.0)
        right = jnp.where(cell < m - 1, right, 0.0)
        results.append(far * up + near * down + line.mid * v + line.side * (left + right))
    return results


def place_of(stage):
    position = lax.axis_index("gy")
    size = 1 << stage
    return (position // size) % 2 == 1, position % size, size


def receive(stage, theta, m, held_in, up_sum, down_sum, first, last):
    upper, place, size = place_of(stage)
    steps = jnp.where(upper, place, size - 1 - place).astype(F32)
    scale = jnp.exp(-theta * (m * steps))
    up, down, before, after = held_in
    return (
        jnp.where(upper, up + scale * up_sum, up),
        jnp.where(upper, down, down + scale * down_sum),
        jnp.where(upper & (place == 0), last, before),
        jnp.where(jnp.logical_not(upper) & (place == size - 1), first, after),
    )


def combine_kernel(stage, last_stage, m, mine, got, *refs):
    if stage:
        held_in, ykeep, _, send, held_out = refs
        before = [held_in[i] for i in range(4)]
    else:
        ykeep, _, send, held_out = refs
        before = [jnp.zeros_like(mine[0])] * 4
    theta = ykeep[4]
    upper, _, size = place_of(stage)
    row, end = got.shape[0] - 1, got.shape[0] - 2 if stage == 0 else got.shape[0] - 1
    lows = (got[0], got[1], got[end], got[row])
    for i, value in enumerate(receive(stage, theta, m, before, *lows)):
        held_out[i] = value
    far = jnp.exp(-theta * (m * size))
    up = jnp.where(upper, mine[0] + far * got[0], got[0] + far * mine[0])
    down = jnp.where(upper, got[1] + far * mine[1], mine[1] + far * got[1])
    _, place, _ = place_of(stage + 1)
    if stage == 0:
        first = jnp.where(upper, got[2], mine[2])
        last = jnp.where(upper, mine[3], got[3])
        halo = jnp.where(place == 0, last, first)
    else:
        halo = got[2]
    if stage + 1 < last_stage:
        send[0] = up
        send[1] = down
        send[2] = halo
    else:
        above, _, _ = place_of(last_stage)
        send[0] = jnp.where(above, down, up)
        send[1] = halo


def arrivals(stage, m, ykeep, got, held_in):
    before = [held_in[i] for i in range(4)]
    return receive(stage, ykeep[4], m, before, got[0], got[0], got[1], got[1])


def middle_kernel(stage, dev_z, bounds, got, held_in, ykeep, zkeep, *refs):
    pieces, sends, sums = refs[: len(bounds) - 1], refs[len(bounds) - 1 : -1], refs[-1]
    m = ykeep.shape[2]
    pos_z = lax.axis_index("gz")
    n = zkeep.shape[2]
    rows = arrivals(stage, m, ykeep, got, held_in)
    totals = []
    for kind in range(4):
        for piece, lo, hi in zip(pieces, bounds, bounds[1:]):
            sums[kind, lo:hi, :] = piece[:, kind, :]
        total = sums[kind]
        for i, row in enumerate(rows):
            if kind < 2:
                amount = jnp.sum(row * zkeep[5 + kind], axis=1, keepdims=True)
            else:
                amount = row[:, :1] if kind == 2 else row[:, n - 1 :]
            total = total + ykeep[i] * amount
        totals.append(total)
    up, down, head, tail = totals
    for by, send in enumerate(sends):
        ahead = pos_z + by + 1 < dev_z
        send[0] = jnp.where(ahead, up, down)
        send[1] = jnp.where(ahead, tail, head)


def held_kernel(stage, dev_z, rates_z, got, held_in, ykeep, zkeep, right_split, right):
    z = Line(down_sublanes(rates_z, right.shape[2]), lax.axis_index("gz"), dev_z, right.shape[2])
    z.vectors()
    for i, row in enumerate(along_lanes(z, arrivals(stage, ykeep.shape[2], ykeep, got, held_in))):
        right[:, i, :] = row
        right[:, 4 + i, :] = zkeep[i]
    b = right[...]
    hi = b.astype(BF16).astype(F32)
    lo = b - hi
    right_split[...] = jnp.concatenate([hi, hi, lo, lo], axis=1).astype(BF16)


def final_kernel(dev_z, bounds, right, ykeep, zkeep, *rest):
    gots, rest = rest[: dev_z - 1], rest[dev_z - 1 :]
    local, (out_hbm, out, out_sems, left) = rest[:-4], rest[-4:]
    planes, m, n = out.shape
    pos_z = lax.axis_index("gz")
    for i in range(4):
        left[:, i, :] = ykeep[i]
    reach = zkeep[4]
    up, down = jnp.zeros_like(gots[0][0]), jnp.zeros_like(gots[0][0])
    scale = jnp.ones_like(reach)
    for by in range(dev_z - 1):
        up = up + jnp.where(pos_z > by, scale * gots[by][0], 0.0)
        behind = gots[dev_z - 2 - by]
        down = down + jnp.where(pos_z + by + 1 < dev_z, scale * behind[0], 0.0)
        scale = scale * reach
    left[:, 4, :] = up
    left[:, 5, :] = down
    left[:, 6, :] = jnp.where(pos_z > 0, gots[0][1], 0.0)
    left[:, 7, :] = jnp.where(pos_z < dev_z - 1, gots[-1][1], 0.0)

    cuts = [planes * c // 16 for c in CUTS]
    stores = []
    for i, (lo, hi) in enumerate(zip(cuts, cuts[1:])):
        for k in range(lo, hi):
            a = left[k]
            a_hi = a.astype(BF16).astype(F32)
            a_lo = a - a_hi
            a = jnp.concatenate([a_hi, a_lo, a_hi, a_lo], axis=0).astype(BF16)
            piece = sum(k >= bound for bound in bounds[1:])
            out[k] = local[piece][k - bounds[piece]] + dot(a, right[k], 0, 0)
        some = pl.ds(lo, hi - lo)
        stores.append(pltpu.make_async_copy(out.at[some], out_hbm.at[some], out_sems.at[i]))
        stores[i].start()
    for store in stores:
        store.wait()


def per_device(x, rates_y, rates_z):
    planes, m, n = x.shape
    dev_y, dev_z = lax.axis_size("gy"), lax.axis_size("gz")
    whole = pl.BlockSpec(memory_space=pltpu.VMEM)

    def params():
        return pltpu.CompilerParams(vmem_limit_bytes=VMEM)

    def cost(flops, moved):
        return pl.CostEstimate(flops=flops, bytes_accessed=moved, transcendentals=0)

    def shape(*dims):
        return jax.ShapeDtypeStruct(dims, F32)

    cells = planes * m * n
    hbm = pl.BlockSpec(memory_space=pltpu.HBM)
    hbm = pl.BlockSpec(memory_space=pltpu.HBM)
    x = pl.pallas_call(
        fetch_kernel,
        in_specs=[hbm],
        out_specs=whole,
        out_shape=shape(planes, m, n),
        scratch_shapes=[pltpu.SemaphoreType.DMA((8,))],
        compiler_params=pltpu.CompilerParams(vmem_limit_bytes=FETCH_VMEM),
        cost_estimate=cost(4, 8 * cells),
        name="fetch",
    )(x)
    send = pl.pallas_call(
        functools.partial(moments_kernel, dev_y),
        in_specs=[whole, whole],
        out_specs=whole,
        out_shape=shape(4, planes, n),
        scratch_shapes=[
            pltpu.VMEM((planes, n), F32),
            pltpu.VMEM((planes, 8, n), F32),
            pltpu.VMEM((planes, 8, n), F32),
        ],
        compiler_params=params(),
        cost_estimate=cost(4 * cells, 4 * cells),
        name="moments",
    )(rates_y, x)
    stages = dev_y.bit_length() - 1
    bounds = [planes * i // stages for i in range(stages + 1)]
    parts, pieces = [], []
    held_in = None
    for stage in range(stages):
        lo, hi = bounds[stage], bounds[stage + 1]
        got = lax.ppermute(send, "gy", [(i, i ^ (1 << stage)) for i in range(dev_y)])
        first = stage == 0
        outs = [shape(hi - lo, m, n), shape(hi - lo, 8, m)]
        if first:
            given = (rates_y, rates_z, x)
            in_specs = [whole] * 3
            outs += [
                shape(5, planes, m),
                shape(7, planes, n),
                shape(7, planes, m),
                shape(8, planes, n),
                shape(planes, 8, n),
            ]
        else:
            given = (x, *tables, send)
            in_specs = [whole] * 5
        part, piece, *rest = pl.pallas_call(
            functools.partial(local_kernel, dev_y, dev_z, lo, hi),
            in_specs=in_specs,
            out_specs=[whole] * len(outs),
            out_shape=outs,
            scratch_shapes=[pltpu.VMEM((2, m, n), F32)],
            compiler_params=params(),
            cost_estimate=cost(12 * (hi - lo) * m * m * n, 8 * (hi - lo) * m * n),
            name="local",
        )(*given)
        parts.append(part)
        pieces.append(piece)
        if first:
            ykeep, zkeep, *tables = rest
        if stage + 1 < stages:
            send, held_in = pl.pallas_call(
                functools.partial(combine_kernel, stage, stages - 1, m),
                in_specs=[whole] * (4 if first else 5),
                out_specs=[whole] * 2,
                out_shape=[shape(3 if stage + 2 < stages else 2, planes, n), shape(4, planes, n)],
                compiler_params=params(),
                cost_estimate=cost(planes * n * 20, planes * n * 64),
                name="combine",
            )(send, got, *(() if first else (held_in,)), ykeep, piece)
    sends = pl.pallas_call(
        functools.partial(middle_kernel, stages - 1, dev_z, bounds),
        in_specs=[whole] * (4 + stages),
        out_specs=[whole] * (dev_z - 1),
        out_shape=[shape(2, planes, m)] * (dev_z - 1),
        scratch_shapes=[pltpu.VMEM((4, planes, m), F32)],
        compiler_params=params(),
        cost_estimate=cost(planes * n * 100, planes * n * 100),
        name="middle",
    )(got, held_in, ykeep, zkeep, *pieces)
    got_z = [
        lax.ppermute(send, "gz", [(i, (i + by + 1) % dev_z) for i in range(dev_z)])
        for by, send in enumerate(sends)
    ]
    held = pl.pallas_call(
        functools.partial(held_kernel, stages - 1, dev_z),
        in_specs=[whole] * 5,
        out_specs=whole,
        out_shape=jax.ShapeDtypeStruct((planes, 32, n), BF16),
        scratch_shapes=[pltpu.VMEM((planes, 8, n), F32)],
        compiler_params=params(),
        cost_estimate=cost(planes * n * 400, planes * n * 100),
        name="held",
    )(rates_z, got, held_in, ykeep, zkeep)
    return pl.pallas_call(
        functools.partial(final_kernel, dev_z, bounds),
        in_specs=[whole] * (dev_z + 2 + stages),
        out_specs=hbm,
        out_shape=shape(planes, m, n),
        scratch_shapes=[
            pltpu.VMEM((planes, m, n), F32),
            pltpu.SemaphoreType.DMA((len(CUTS) - 1,)),
            pltpu.VMEM((planes, 8, m), F32),
        ],
        compiler_params=params(),
        cost_estimate=cost(64 * cells, 8 * cells),
        name="final",
    )(held, ykeep, zkeep, *got_z, *parts)


def solution(mesh):
    return jax.shard_map(
        per_device,
        mesh=mesh,
        in_specs=(P(None, "gy", "gz"), P(), P()),
        out_specs=P(None, "gy", "gz"),
        check_vma=False,
    )
```

```python
import functools

import jax
import jax.numpy as jnp
from jax import lax
from jax.experimental import pallas as pl
from jax.experimental.pallas import tpu as pltpu
from jax.sharding import PartitionSpec as P

alpha = 2.0 / 11.0
inner_weight = 12.0 / 11.0
outer_weight = 3.0 / 44.0
F32 = jnp.float32
BF16 = jnp.bfloat16
VMEM = 24 * 1024 * 1024
FETCH_VMEM = 50 * 1024 * 1024
CUTS = (0, 2, 5, 10, 16)


def down_sublanes(rates, lanes):
    planes = rates.shape[0]
    row = jnp.broadcast_to(rates[...].reshape(1, planes), (planes, planes))
    diagonal = lax.broadcasted_iota(jnp.int32, row.shape, 0) == lax.broadcasted_iota(
        jnp.int32, row.shape, 1
    )
    column = jnp.sum(jnp.where(diagonal, row, 0.0), axis=1, keepdims=True)
    return jnp.broadcast_to(column, (planes, lanes))


class Line:
    def __init__(self, rate, position, devices, m):
        beside = inner_weight * rate - alpha
        eps = (1.0 + 2.0 * alpha) / (2.0 * beside)
        sinh = jnp.sqrt(eps * (2.0 + eps))
        corner = rate * outer_weight
        self.m = m
        self.growth = 1.0 + (eps + sinh)
        self.theta = jnp.log1p(eps + sinh)
        total = m * devices
        self.far = total + 1 - m * position
        self.near = m * position
        self.c = m // 2
        self.green = 1.0 / (2.0 * beside * sinh * (1.0 - self.power(2 * (total + 1))))
        self.rho = 1.0 + 2.0 * alpha * (1.0 + eps) + 4.0 * corner * eps * (2.0 + eps)
        self.side = -corner / beside
        self.mid = 2.0 * self.side * (1.0 + eps) - alpha / beside
        self.corner = corner
        self.is_first = jnp.where(position == 0, 1.0, 0.0).astype(F32)
        self.is_last = jnp.where(position == devices - 1, 1.0, 0.0).astype(F32)
        self.cell = lax.broadcasted_iota(jnp.int32, rate.shape, 1)

    def power(self, n):
        return jnp.exp(-self.theta * jnp.asarray(n, F32))

    def vectors(self):
        i = (self.cell + (1 - self.c)).astype(F32)
        down, up = jnp.exp(-self.theta * i), jnp.exp(self.theta * i)
        self.cut_far = self.power(2 * (self.far - self.c))
        self.cut_near = self.power(2 * (self.near + self.c))
        self.phi = down - self.cut_far * up
        self.chi = up - self.cut_near * down
        self.ends = jnp.where(self.cell == 0, self.is_first, 0.0) + jnp.where(
            self.cell == self.m - 1, self.is_last, 0.0
        )
        self.weight = self.green * (self.rho + self.corner * self.ends)
        self.send_up = self.weight * self.chi * self.power(self.m - self.c)
        self.send_down = self.weight * self.phi * self.power(self.c - 1)
        self.get_up = self.phi * self.power(self.c)
        self.get_down = self.chi * self.power(self.m + 1 - self.c)
        self.head = jnp.where(self.cell == 0, 1.0, 0.0).astype(F32)
        self.tail = jnp.where(self.cell == self.m - 1, 1.0, 0.0).astype(F32)


def split(a):
    hi = a.astype(BF16)
    return hi, (a - hi.astype(F32)).astype(BF16)


def dot(a, b, ca, cb):
    return lax.dot_general(a, b, (((ca,), (cb,)), ((), ())), preferred_element_type=F32)


def product(a_hi, a_lo, b_hi, b_lo):
    b = jnp.concatenate([b_hi, b_lo], axis=1)
    n = b_hi.shape[1]
    both = dot(jnp.concatenate([a_hi, a_lo], axis=1), jnp.concatenate([b, b], axis=0), 1, 0)
    return both[:, :n] + both[:, n:]


def fetch_kernel(x_hbm, x, sems):
    parts = sems.shape[0]
    group = x.shape[0] // parts
    copies = []
    for i in range(parts):
        some = pl.ds(i * group, group)
        copies.append(pltpu.make_async_copy(x_hbm.at[some], x.at[some], sems.at[i]))
        copies[i].start()
    for copy in copies:
        copy.wait()


def moments_kernel(devices, rates, x, out, table, up_rows, down_rows):
    planes, m, n = x.shape
    position = lax.axis_index("gy")
    line = Line(down_sublanes(rates, n), position, devices, m)
    one = 1.0 / line.growth
    eighth = one * one
    eighth = eighth * eighth
    eighth = eighth * eighth
    across = line.power(m - 1)
    lower_scale, upper_scale = line.corner * line.is_first, line.corner * line.is_last
    turn_up, turn_down = line.power(2 * line.near + m + 1), line.power(2 * line.far - m - 1)
    table[...] = eighth
    for k in range(planes):
        ratio = jnp.broadcast_to(table[k : k + 1, :], (8, n))
        rows = [x[k, v : v + 8, :] for v in range(0, m, 8)]
        up, down = rows[0], rows[-1]
        for ahead, behind in zip(rows[1:], rows[-2::-1]):
            up = up * ratio + ahead
            down = down * ratio + behind
        up_rows[k] = up
        down_rows[k] = down
    up, down = up_rows[:, 0, :], down_rows[:, 7, :]
    for s in range(1, 8):
        up = up * one + up_rows[:, s, :]
        down = down * one + down_rows[:, 7 - s, :]
    first, last = x[:, 0, :], x[:, m - 1, :]
    lower, upper = lower_scale * first, upper_scale * last
    up = line.rho * up + across * lower + upper
    down = line.rho * down + lower + across * upper
    going_up = line.green * (up - turn_up * down)
    going_down = line.green * (down - turn_down * up)
    out[0] = going_up
    out[1] = going_down
    out[2] = first
    out[3] = last


def columns(theta, cut_far, cut_near, m):
    shape = (8, theta.shape[1])
    i = (lax.broadcasted_iota(jnp.int32, shape, 0) + (1 - m // 2)).astype(F32)
    down, up = jnp.exp(-theta * i), jnp.exp(theta * i)
    grow, fall = jnp.exp(theta * 8.0), jnp.exp(theta * -8.0)
    phi, chi = [], []
    for _ in range(m // 8):
        phi.append(down - cut_far * up)
        chi.append(up - cut_near * down)
        down, up = down * fall, up * grow
    return phi, chi


def make_tables(dev_y, dev_z, rates_y, rates_z, m, n, ykeep, zkeep, ytab, ztab, nz):
    pos_y, pos_z = lax.axis_index("gy"), lax.axis_index("gz")
    y = Line(down_sublanes(rates_y, m), pos_y, dev_y, m)
    y.vectors()
    for i, row in enumerate((y.get_up, y.get_down, y.side * y.head, y.side * y.tail, y.theta)):
        ykeep[i] = row
    for i, row in enumerate(
        (y.theta, y.cut_far, y.cut_near, y.phi * y.weight, y.chi * y.weight, y.mid, y.side)
    ):
        ytab[i] = row
    z = Line(down_sublanes(rates_z, n), pos_z, dev_z, n)
    z.vectors()
    for i, row in enumerate(
        (z.get_up, z.get_down, z.side * z.head, z.side * z.tail, z.power(n), z.send_up, z.send_down)
    ):
        zkeep[i] = row
    base = z.green * z.rho
    for i, row in enumerate(
        (z.theta, z.cut_far, z.cut_near, z.phi * base, z.chi * base, z.mid, z.side, z.corner / z.rho)
    ):
        ztab[i] = row
    for i, row in enumerate((z.send_up, z.send_down, z.head, z.tail)):
        nz[:, i, :] = row
        nz[:, 4 + i, :] = jnp.zeros_like(row)


def local_kernel(dev_y, dev_z, lo, hi, *refs):
    if lo == 0:
        rates_y, rates_z, x, out, sums, ykeep, zkeep, ytab, ztab, nz = refs[:10]
        make_tables(
            dev_y, dev_z, rates_y, rates_z, x.shape[1], x.shape[2], ykeep, zkeep, ytab, ztab, nz
        )
    else:
        x, ytab, ztab, nz, _, out, sums = refs[:7]
    band = refs[-1]
    m, n = x.shape[1:]
    pos_z = lax.axis_index("gz")
    r = lax.broadcasted_iota(jnp.int32, (m, n), 0)
    c = lax.broadcasted_iota(jnp.int32, (m, n), 1)
    band[0] = jnp.where(r == c, 1.0, 0.0)
    band[1] = jnp.where((r == c + 1) | (r + 1 == c), 1.0, 0.0)
    z_first = jnp.where(pos_z == 0, 1.0, 0.0).astype(F32)
    z_last = jnp.where(pos_z == dev_z - 1, 1.0, 0.0).astype(F32)
    sub = lax.broadcasted_iota(jnp.int32, (8, n), 0)
    at_head = jnp.where(sub == 0, z_first, 0.0)
    at_tail = jnp.where(sub == 7, z_last, 0.0)

    for k in range(lo, hi):
        g = k - lo

        def rows(ref, i):
            return ref[i, k : k + 1, :]

        phi, chi = columns(rows(ytab, 0), rows(ytab, 1), rows(ytab, 2), m)
        phi_row, chi_row, mid, side = [rows(ytab, i) for i in (3, 4, 5, 6)]
        dmat = jnp.concatenate(
            [
                jnp.minimum(phi[v] * chi_row, chi[v] * phi_row)
                + mid * band[0, 8 * v : 8 * v + 8, :]
                + side * band[1, 8 * v : 8 * v + 8, :]
                for v in range(m // 8)
            ],
            axis=0,
        )
        d_hi, d_lo = split(dmat)
        x_hi, x_lo = split(x[k])
        turned = product(d_hi, d_lo, x_hi, x_lo)
        t_hi, t_lo = split(turned)

        phi, chi = columns(rows(ztab, 0), rows(ztab, 1), rows(ztab, 2), n)
        phi_row, chi_row, mid, side, edge = [rows(ztab, i) for i in (3, 4, 5, 6, 7)]
        head, tail = 1.0 + edge * at_head, 1.0 + edge * at_tail
        phi[0], chi[0] = phi[0] * head, chi[0] * head
        phi[-1], chi[-1] = phi[-1] * tail, chi[-1] * tail
        bmat = jnp.concatenate(
            [
                jnp.minimum(phi[v] * chi_row, chi[v] * phi_row)
                + mid * band[0, 8 * v : 8 * v + 8, :]
                + side * band[1, 8 * v : 8 * v + 8, :]
                for v in range(n // 8)
            ],
            axis=0,
        )
        b_hi, b_lo = split(bmat)
        out[g] = product(t_hi, t_lo, b_hi, b_lo)
        functionals = nz[k]
        f_hi = functionals.astype(BF16).astype(F32)
        f16 = jnp.concatenate([f_hi, functionals - f_hi], axis=0).astype(BF16)
        both = dot(
            jnp.concatenate([f16, f16], axis=1), jnp.concatenate([t_hi, t_lo], axis=1), 1, 1
        )
        sums[g] = both[:8] + both[8:]


def along_lanes(line, f):
    m = line.m
    cell = line.cell
    near = 1.0 - line.power(2 * line.near) * jnp.exp(-2.0 * line.theta * (cell + 1).astype(F32))
    far = 1.0 - line.power(2 * (line.far - m - 1)) * jnp.exp(
        -2.0 * line.theta * (m - cell).astype(F32)
    )
    ups, downs = [], []
    span = 1
    while span < m:
        ratio = line.power(span)
        ups.append((span, jnp.where(cell >= span, ratio, 0.0)))
        downs.append((m - span, jnp.where(cell < m - span, ratio, 0.0)))
        span *= 2
    results = []
    for v in f:
        source = line.weight * v
        up, start = near * source, far * source
        for shift, ratio in ups:
            up = up + ratio * pltpu.roll(up, shift, 1)
        down = start
        for shift, ratio in downs:
            down = down + ratio * pltpu.roll(down, shift, 1)
        down = down - start
        left, right = pltpu.roll(v, 1, 1), pltpu.roll(v, m - 1, 1)
        left = jnp.where(cell > 0, left, 0.0)
        right = jnp.where(cell < m - 1, right, 0.0)
        results.append(far * up + near * down + line.mid * v + line.side * (left + right))
    return results


def place_of(stage):
    position = lax.axis_index("gy")
    size = 1 << stage
    return (position // size) % 2 == 1, position % size, size


def receive(stage, theta, m, held_in, up_sum, down_sum, first, last):
    upper, place, size = place_of(stage)
    steps = jnp.where(upper, place, size - 1 - place).astype(F32)
    scale = jnp.exp(-theta * (m * steps))
    up, down, before, after = held_in
    return (
        jnp.where(upper, up + scale * up_sum, up),
        jnp.where(upper, down, down + scale * down_sum),
        jnp.where(upper & (place == 0), last, before),
        jnp.where(jnp.logical_not(upper) & (place == size - 1), first, after),
    )


def combine_kernel(stage, last_stage, m, mine, got, *refs):
    if stage:
        held_in, ykeep, _, send, held_out = refs
        before = [held_in[i] for i in range(4)]
    else:
        ykeep, _, send, held_out = refs
        before = [jnp.zeros_like(mine[0])] * 4
    theta = ykeep[4]
    upper, _, size = place_of(stage)
    row, end = got.shape[0] - 1, got.shape[0] - 2 if stage == 0 else got.shape[0] - 1
    lows = (got[0], got[1], got[end], got[row])
    for i, value in enumerate(receive(stage, theta, m, before, *lows)):
        held_out[i] = value
    far = jnp.exp(-theta * (m * size))
    up = jnp.where(upper, mine[0] + far * got[0], got[0] + far * mine[0])
    down = jnp.where(upper, got[1] + far * mine[1], mine[1] + far * got[1])
    _, place, _ = place_of(stage + 1)
    if stage == 0:
        first = jnp.where(upper, got[2], mine[2])
        last = jnp.where(upper, mine[3], got[3])
        halo = jnp.where(place == 0, last, first)
    else:
        halo = got[2]
    if stage + 1 < last_stage:
        send[0] = up
        send[1] = down
        send[2] = halo
    else:
        above, _, _ = place_of(last_stage)
        send[0] = jnp.where(above, down, up)
        send[1] = halo


def arrivals(stage, m, ykeep, got, held_in):
    before = [held_in[i] for i in range(4)]
    return receive(stage, ykeep[4], m, before, got[0], got[0], got[1], got[1])


def middle_kernel(stage, dev_z, bounds, got, held_in, ykeep, zkeep, *refs):
    pieces, sends, sums = refs[: len(bounds) - 1], refs[len(bounds) - 1 : -1], refs[-1]
    m = ykeep.shape[2]
    pos_z = lax.axis_index("gz")
    n = zkeep.shape[2]
    rows = arrivals(stage, m, ykeep, got, held_in)
    totals = []
    for kind in range(4):
        for piece, lo, hi in zip(pieces, bounds, bounds[1:]):
            sums[kind, lo:hi, :] = piece[:, kind, :]
        total = sums[kind]
        for i, row in enumerate(rows):
            if kind < 2:
                amount = jnp.sum(row * zkeep[5 + kind], axis=1, keepdims=True)
            else:
                amount = row[:, :1] if kind == 2 else row[:, n - 1 :]
            total = total + ykeep[i] * amount
        totals.append(total)
    up, down, head, tail = totals
    for by, send in enumerate(sends):
        ahead = pos_z + by + 1 < dev_z
        send[0] = jnp.where(ahead, up, down)
        send[1] = jnp.where(ahead, tail, head)


def held_kernel(stage, dev_z, rates_z, got, held_in, ykeep, zkeep, right_split, right):
    z = Line(down_sublanes(rates_z, right.shape[2]), lax.axis_index("gz"), dev_z, right.shape[2])
    z.vectors()
    for i, row in enumerate(along_lanes(z, arrivals(stage, ykeep.shape[2], ykeep, got, held_in))):
        right[:, i, :] = row
        right[:, 4 + i, :] = zkeep[i]
    b = right[...]
    hi = b.astype(BF16).astype(F32)
    lo = b - hi
    right_split[...] = jnp.concatenate([hi, hi, lo, lo], axis=1).astype(BF16)


def final_kernel(dev_z, bounds, right, ykeep, zkeep, *rest):
    gots, rest = rest[: dev_z - 1], rest[dev_z - 1 :]
    local, (out_hbm, out, out_sems, left) = rest[:-4], rest[-4:]
    planes, m, n = out.shape
    pos_z = lax.axis_index("gz")
    for i in range(4):
        left[:, i, :] = ykeep[i]
    reach = zkeep[4]
    up, down = jnp.zeros_like(gots[0][0]), jnp.zeros_like(gots[0][0])
    scale = jnp.ones_like(reach)
    for by in range(dev_z - 1):
        up = up + jnp.where(pos_z > by, scale * gots[by][0], 0.0)
        behind = gots[dev_z - 2 - by]
        down = down + jnp.where(pos_z + by + 1 < dev_z, scale * behind[0], 0.0)
        scale = scale * reach
    left[:, 4, :] = up
    left[:, 5, :] = down
    left[:, 6, :] = jnp.where(pos_z > 0, gots[0][1], 0.0)
    left[:, 7, :] = jnp.where(pos_z < dev_z - 1, gots[-1][1], 0.0)

    cuts = [planes * c // 16 for c in CUTS]
    stores = []
    for i, (lo, hi) in enumerate(zip(cuts, cuts[1:])):
        for k in range(lo, hi):
            a = left[k]
            a_hi = a.astype(BF16).astype(F32)
            a_lo = a - a_hi
            a = jnp.concatenate([a_hi, a_lo, a_hi, a_lo], axis=0).astype(BF16)
            piece = sum(k >= bound for bound in bounds[1:])
            out[k] = local[piece][k - bounds[piece]] + dot(a, right[k], 0, 0)
        some = pl.ds(lo, hi - lo)
        stores.append(pltpu.make_async_copy(out.at[some], out_hbm.at[some], out_sems.at[i]))
        stores[i].start()
    for store in stores:
        store.wait()


def per_device(x, rates_y, rates_z):
    planes, m, n = x.shape
    dev_y, dev_z = lax.axis_size("gy"), lax.axis_size("gz")
    whole = pl.BlockSpec(memory_space=pltpu.VMEM)

    def params():
        return pltpu.CompilerParams(vmem_limit_bytes=VMEM)

    def cost(flops, moved):
        return pl.CostEstimate(flops=flops, bytes_accessed=moved, transcendentals=0)

    def shape(*dims):
        return jax.ShapeDtypeStruct(dims, F32)

    cells = planes * m * n
    hbm = pl.BlockSpec(memory_space=pltpu.HBM)
    hbm = pl.BlockSpec(memory_space=pltpu.HBM)
    x = pl.pallas_call(
        fetch_kernel,
        in_specs=[hbm],
        out_specs=whole,
        out_shape=shape(planes, m, n),
        scratch_shapes=[pltpu.SemaphoreType.DMA((2,))],
        compiler_params=pltpu.CompilerParams(vmem_limit_bytes=FETCH_VMEM),
        cost_estimate=cost(4, 8 * cells),
        name="fetch",
    )(x)
    send = pl.pallas_call(
        functools.partial(moments_kernel, dev_y),
        in_specs=[whole, whole],
        out_specs=whole,
        out_shape=shape(4, planes, n),
        scratch_shapes=[
            pltpu.VMEM((planes, n), F32),
            pltpu.VMEM((planes, 8, n), F32),
            pltpu.VMEM((planes, 8, n), F32),
        ],
        compiler_params=params(),
        cost_estimate=cost(4 * cells, 4 * cells),
        name="moments",
    )(rates_y, x)
    stages = dev_y.bit_length() - 1
    bounds = [planes * i // stages for i in range(stages + 1)]
    parts, pieces = [], []
    held_in = None
    for stage in range(stages):
        lo, hi = bounds[stage], bounds[stage + 1]
        got = lax.ppermute(send, "gy", [(i, i ^ (1 << stage)) for i in range(dev_y)])
        first = stage == 0
        outs = [shape(hi - lo, m, n), shape(hi - lo, 8, m)]
        if first:
            given = (rates_y, rates_z, x)
            in_specs = [whole] * 3
            outs += [
                shape(5, planes, m),
                shape(7, planes, n),
                shape(7, planes, m),
                shape(8, planes, n),
                shape(planes, 8, n),
            ]
        else:
            given = (x, *tables, send)
            in_specs = [whole] * 5
        part, piece, *rest = pl.pallas_call(
            functools.partial(local_kernel, dev_y, dev_z, lo, hi),
            in_specs=in_specs,
            out_specs=[whole] * len(outs),
            out_shape=outs,
            scratch_shapes=[pltpu.VMEM((2, m, n), F32)],
            compiler_params=params(),
            cost_estimate=cost(12 * (hi - lo) * m * m * n, 8 * (hi - lo) * m * n),
            name="local",
        )(*given)
        parts.append(part)
        pieces.append(piece)
        if first:
            ykeep, zkeep, *tables = rest
        if stage + 1 < stages:
            send, held_in = pl.pallas_call(
                functools.partial(combine_kernel, stage, stages - 1, m),
                in_specs=[whole] * (4 if first else 5),
                out_specs=[whole] * 2,
                out_shape=[shape(3 if stage + 2 < stages else 2, planes, n), shape(4, planes, n)],
                compiler_params=params(),
                cost_estimate=cost(planes * n * 20, planes * n * 64),
                name="combine",
            )(send, got, *(() if first else (held_in,)), ykeep, piece)
    sends = pl.pallas_call(
        functools.partial(middle_kernel, stages - 1, dev_z, bounds),
        in_specs=[whole] * (4 + stages),
        out_specs=[whole] * (dev_z - 1),
        out_shape=[shape(2, planes, m)] * (dev_z - 1),
        scratch_shapes=[pltpu.VMEM((4, planes, m), F32)],
        compiler_params=params(),
        cost_estimate=cost(planes * n * 100, planes * n * 100),
        name="middle",
    )(got, held_in, ykeep, zkeep, *pieces)
    got_z = [
        lax.ppermute(send, "gz", [(i, (i + by + 1) % dev_z) for i in range(dev_z)])
        for by, send in enumerate(sends)
    ]
    held = pl.pallas_call(
        functools.partial(held_kernel, stages - 1, dev_z),
        in_specs=[whole] * 5,
        out_specs=whole,
        out_shape=jax.ShapeDtypeStruct((planes, 32, n), BF16),
        scratch_shapes=[pltpu.VMEM((planes, 8, n), F32)],
        compiler_params=params(),
        cost_estimate=cost(planes * n * 400, planes * n * 100),
        name="held",
    )(rates_z, got, held_in, ykeep, zkeep)
    return pl.pallas_call(
        functools.partial(final_kernel, dev_z, bounds),
        in_specs=[whole] * (dev_z + 2 + stages),
        out_specs=hbm,
        out_shape=shape(planes, m, n),
        scratch_shapes=[
            pltpu.VMEM((planes, m, n), F32),
            pltpu.SemaphoreType.DMA((len(CUTS) - 1,)),
            pltpu.VMEM((planes, 8, m), F32),
        ],
        compiler_params=params(),
        cost_estimate=cost(64 * cells, 8 * cells),
        name="final",
    )(held, ykeep, zkeep, *got_z, *parts)


def solution(mesh):
    return jax.shard_map(
        per_device,
        mesh=mesh,
        in_specs=(P(None, "gy", "gz"), P(), P()),
        out_specs=P(None, "gy", "gz"),
        check_vma=False,
    )
```

```python
import functools

import jax
import jax.numpy as jnp
from jax import lax
from jax.experimental import pallas as pl
from jax.experimental.pallas import tpu as pltpu
from jax.sharding import PartitionSpec as P

alpha = 2.0 / 11.0
inner_weight = 12.0 / 11.0
outer_weight = 3.0 / 44.0
F32 = jnp.float32
BF16 = jnp.bfloat16
VMEM = 24 * 1024 * 1024
FETCH_VMEM = 50 * 1024 * 1024
CUTS = (0, 1, 3, 6, 11, 16)


def down_sublanes(rates, lanes):
    planes = rates.shape[0]
    row = jnp.broadcast_to(rates[...].reshape(1, planes), (planes, planes))
    diagonal = lax.broadcasted_iota(jnp.int32, row.shape, 0) == lax.broadcasted_iota(
        jnp.int32, row.shape, 1
    )
    column = jnp.sum(jnp.where(diagonal, row, 0.0), axis=1, keepdims=True)
    return jnp.broadcast_to(column, (planes, lanes))


class Line:
    def __init__(self, rate, position, devices, m):
        beside = inner_weight * rate - alpha
        eps = (1.0 + 2.0 * alpha) / (2.0 * beside)
        sinh = jnp.sqrt(eps * (2.0 + eps))
        corner = rate * outer_weight
        self.m = m
        self.growth = 1.0 + (eps + sinh)
        self.theta = jnp.log1p(eps + sinh)
        total = m * devices
        self.far = total + 1 - m * position
        self.near = m * position
        self.c = m // 2
        self.green = 1.0 / (2.0 * beside * sinh * (1.0 - self.power(2 * (total + 1))))
        self.rho = 1.0 + 2.0 * alpha * (1.0 + eps) + 4.0 * corner * eps * (2.0 + eps)
        self.side = -corner / beside
        self.mid = 2.0 * self.side * (1.0 + eps) - alpha / beside
        self.corner = corner
        self.is_first = jnp.where(position == 0, 1.0, 0.0).astype(F32)
        self.is_last = jnp.where(position == devices - 1, 1.0, 0.0).astype(F32)
        self.cell = lax.broadcasted_iota(jnp.int32, rate.shape, 1)

    def power(self, n):
        return jnp.exp(-self.theta * jnp.asarray(n, F32))

    def vectors(self):
        i = (self.cell + (1 - self.c)).astype(F32)
        down, up = jnp.exp(-self.theta * i), jnp.exp(self.theta * i)
        self.cut_far = self.power(2 * (self.far - self.c))
        self.cut_near = self.power(2 * (self.near + self.c))
        self.phi = down - self.cut_far * up
        self.chi = up - self.cut_near * down
        self.ends = jnp.where(self.cell == 0, self.is_first, 0.0) + jnp.where(
            self.cell == self.m - 1, self.is_last, 0.0
        )
        self.weight = self.green * (self.rho + self.corner * self.ends)
        self.send_up = self.weight * self.chi * self.power(self.m - self.c)
        self.send_down = self.weight * self.phi * self.power(self.c - 1)
        self.get_up = self.phi * self.power(self.c)
        self.get_down = self.chi * self.power(self.m + 1 - self.c)
        self.head = jnp.where(self.cell == 0, 1.0, 0.0).astype(F32)
        self.tail = jnp.where(self.cell == self.m - 1, 1.0, 0.0).astype(F32)


def split(a):
    hi = a.astype(BF16)
    return hi, (a - hi.astype(F32)).astype(BF16)


def dot(a, b, ca, cb):
    return lax.dot_general(a, b, (((ca,), (cb,)), ((), ())), preferred_element_type=F32)


def product(a_hi, a_lo, b_hi, b_lo):
    b = jnp.concatenate([b_hi, b_lo], axis=1)
    n = b_hi.shape[1]
    both = dot(jnp.concatenate([a_hi, a_lo], axis=1), jnp.concatenate([b, b], axis=0), 1, 0)
    return both[:, :n] + both[:, n:]


def fetch_kernel(x_hbm, x, sems):
    parts = sems.shape[0]
    group = x.shape[0] // parts
    copies = []
    for i in range(parts):
        some = pl.ds(i * group, group)
        copies.append(pltpu.make_async_copy(x_hbm.at[some], x.at[some], sems.at[i]))
        copies[i].start()
    for copy in copies:
        copy.wait()


def moments_kernel(devices, rates, x, out, table, up_rows, down_rows):
    planes, m, n = x.shape
    position = lax.axis_index("gy")
    line = Line(down_sublanes(rates, n), position, devices, m)
    one = 1.0 / line.growth
    eighth = one * one
    eighth = eighth * eighth
    eighth = eighth * eighth
    across = line.power(m - 1)
    lower_scale, upper_scale = line.corner * line.is_first, line.corner * line.is_last
    turn_up, turn_down = line.power(2 * line.near + m + 1), line.power(2 * line.far - m - 1)
    table[...] = eighth
    for k in range(planes):
        ratio = jnp.broadcast_to(table[k : k + 1, :], (8, n))
        rows = [x[k, v : v + 8, :] for v in range(0, m, 8)]
        up, down = rows[0], rows[-1]
        for ahead, behind in zip(rows[1:], rows[-2::-1]):
            up = up * ratio + ahead
            down = down * ratio + behind
        up_rows[k] = up
        down_rows[k] = down
    up, down = up_rows[:, 0, :], down_rows[:, 7, :]
    for s in range(1, 8):
        up = up * one + up_rows[:, s, :]
        down = down * one + down_rows[:, 7 - s, :]
    first, last = x[:, 0, :], x[:, m - 1, :]
    lower, upper = lower_scale * first, upper_scale * last
    up = line.rho * up + across * lower + upper
    down = line.rho * down + lower + across * upper
    going_up = line.green * (up - turn_up * down)
    going_down = line.green * (down - turn_down * up)
    out[0] = going_up
    out[1] = going_down
    out[2] = first
    out[3] = last


def columns(theta, cut_far, cut_near, m):
    shape = (8, theta.shape[1])
    i = (lax.broadcasted_iota(jnp.int32, shape, 0) + (1 - m // 2)).astype(F32)
    down, up = jnp.exp(-theta * i), jnp.exp(theta * i)
    grow, fall = jnp.exp(theta * 8.0), jnp.exp(theta * -8.0)
    phi, chi = [], []
    for _ in range(m // 8):
        phi.append(down - cut_far * up)
        chi.append(up - cut_near * down)
        down, up = down * fall, up * grow
    return phi, chi


def make_tables(dev_y, dev_z, rates_y, rates_z, m, n, ykeep, zkeep, ytab, ztab, nz):
    pos_y, pos_z = lax.axis_index("gy"), lax.axis_index("gz")
    y = Line(down_sublanes(rates_y, m), pos_y, dev_y, m)
    y.vectors()
    for i, row in enumerate((y.get_up, y.get_down, y.side * y.head, y.side * y.tail, y.theta)):
        ykeep[i] = row
    for i, row in enumerate(
        (y.theta, y.cut_far, y.cut_near, y.phi * y.weight, y.chi * y.weight, y.mid, y.side)
    ):
        ytab[i] = row
    z = Line(down_sublanes(rates_z, n), pos_z, dev_z, n)
    z.vectors()
    for i, row in enumerate(
        (z.get_up, z.get_down, z.side * z.head, z.side * z.tail, z.power(n), z.send_up, z.send_down)
    ):
        zkeep[i] = row
    base = z.green * z.rho
    for i, row in enumerate(
        (z.theta, z.cut_far, z.cut_near, z.phi * base, z.chi * base, z.mid, z.side, z.corner / z.rho)
    ):
        ztab[i] = row
    for i, row in enumerate((z.send_up, z.send_down, z.head, z.tail)):
        nz[:, i, :] = row
        nz[:, 4 + i, :] = jnp.zeros_like(row)


def local_kernel(dev_y, dev_z, lo, hi, *refs):
    if lo == 0:
        rates_y, rates_z, x, out, sums, ykeep, zkeep, ytab, ztab, nz = refs[:10]
        make_tables(
            dev_y, dev_z, rates_y, rates_z, x.shape[1], x.shape[2], ykeep, zkeep, ytab, ztab, nz
        )
    else:
        x, ytab, ztab, nz, _, out, sums = refs[:7]
    band = refs[-1]
    m, n = x.shape[1:]
    pos_z = lax.axis_index("gz")
    r = lax.broadcasted_iota(jnp.int32, (m, n), 0)
    c = lax.broadcasted_iota(jnp.int32, (m, n), 1)
    band[0] = jnp.where(r == c, 1.0, 0.0)
    band[1] = jnp.where((r == c + 1) | (r + 1 == c), 1.0, 0.0)
    z_first = jnp.where(pos_z == 0, 1.0, 0.0).astype(F32)
    z_last = jnp.where(pos_z == dev_z - 1, 1.0, 0.0).astype(F32)
    sub = lax.broadcasted_iota(jnp.int32, (8, n), 0)
    at_head = jnp.where(sub == 0, z_first, 0.0)
    at_tail = jnp.where(sub == 7, z_last, 0.0)

    for k in range(lo, hi):
        g = k - lo

        def rows(ref, i):
            return ref[i, k : k + 1, :]

        phi, chi = columns(rows(ytab, 0), rows(ytab, 1), rows(ytab, 2), m)
        phi_row, chi_row, mid, side = [rows(ytab, i) for i in (3, 4, 5, 6)]
        dmat = jnp.concatenate(
            [
                jnp.minimum(phi[v] * chi_row, chi[v] * phi_row)
                + mid * band[0, 8 * v : 8 * v + 8, :]
                + side * band[1, 8 * v : 8 * v + 8, :]
                for v in range(m // 8)
            ],
            axis=0,
        )
        d_hi, d_lo = split(dmat)
        x_hi, x_lo = split(x[k])
        turned = product(d_hi, d_lo, x_hi, x_lo)
        t_hi, t_lo = split(turned)

        phi, chi = columns(rows(ztab, 0), rows(ztab, 1), rows(ztab, 2), n)
        phi_row, chi_row, mid, side, edge = [rows(ztab, i) for i in (3, 4, 5, 6, 7)]
        head, tail = 1.0 + edge * at_head, 1.0 + edge * at_tail
        phi[0], chi[0] = phi[0] * head, chi[0] * head
        phi[-1], chi[-1] = phi[-1] * tail, chi[-1] * tail
        bmat = jnp.concatenate(
            [
                jnp.minimum(phi[v] * chi_row, chi[v] * phi_row)
                + mid * band[0, 8 * v : 8 * v + 8, :]
                + side * band[1, 8 * v : 8 * v + 8, :]
                for v in range(n // 8)
            ],
            axis=0,
        )
        b_hi, b_lo = split(bmat)
        out[g] = product(t_hi, t_lo, b_hi, b_lo)
        functionals = nz[k]
        f_hi = functionals.astype(BF16).astype(F32)
        f16 = jnp.concatenate([f_hi, functionals - f_hi], axis=0).astype(BF16)
        both = dot(
            jnp.concatenate([f16, f16], axis=1), jnp.concatenate([t_hi, t_lo], axis=1), 1, 1
        )
        sums[g] = both[:8] + both[8:]


def along_lanes(line, f):
    m = line.m
    cell = line.cell
    near = 1.0 - line.power(2 * line.near) * jnp.exp(-2.0 * line.theta * (cell + 1).astype(F32))
    far = 1.0 - line.power(2 * (line.far - m - 1)) * jnp.exp(
        -2.0 * line.theta * (m - cell).astype(F32)
    )
    ups, downs = [], []
    span = 1
    while span < m:
        ratio = line.power(span)
        ups.append((span, jnp.where(cell >= span, ratio, 0.0)))
        downs.append((m - span, jnp.where(cell < m - span, ratio, 0.0)))
        span *= 2
    results = []
    for v in f:
        source = line.weight * v
        up, start = near * source, far * source
        for shift, ratio in ups:
            up = up + ratio * pltpu.roll(up, shift, 1)
        down = start
        for shift, ratio in downs:
            down = down + ratio * pltpu.roll(down, shift, 1)
        down = down - start
        left, right = pltpu.roll(v, 1, 1), pltpu.roll(v, m - 1, 1)
        left = jnp.where(cell > 0, left, 0.0)
        right = jnp.where(cell < m - 1, right, 0.0)
        results.append(far * up + near * down + line.mid * v + line.side * (left + right))
    return results


def place_of(stage):
    position = lax.axis_index("gy")
    size = 1 << stage
    return (position // size) % 2 == 1, position % size, size


def receive(stage, theta, m, held_in, up_sum, down_sum, first, last):
    upper, place, size = place_of(stage)
    steps = jnp.where(upper, place, size - 1 - place).astype(F32)
    scale = jnp.exp(-theta * (m * steps))
    up, down, before, after = held_in
    return (
        jnp.where(upper, up + scale * up_sum, up),
        jnp.where(upper, down, down + scale * down_sum),
        jnp.where(upper & (place == 0), last, before),
        jnp.where(jnp.logical_not(upper) & (place == size - 1), first, after),
    )


def combine_kernel(stage, last_stage, m, mine, got, *refs):
    if stage:
        held_in, ykeep, _, send, held_out = refs
        before = [held_in[i] for i in range(4)]
    else:
        ykeep, _, send, held_out = refs
        before = [jnp.zeros_like(mine[0])] * 4
    theta = ykeep[4]
    upper, _, size = place_of(stage)
    row, end = got.shape[0] - 1, got.shape[0] - 2 if stage == 0 else got.shape[0] - 1
    lows = (got[0], got[1], got[end], got[row])
    for i, value in enumerate(receive(stage, theta, m, before, *lows)):
        held_out[i] = value
    far = jnp.exp(-theta * (m * size))
    up = jnp.where(upper, mine[0] + far * got[0], got[0] + far * mine[0])
    down = jnp.where(upper, got[1] + far * mine[1], mine[1] + far * got[1])
    _, place, _ = place_of(stage + 1)
    if stage == 0:
        first = jnp.where(upper, got[2], mine[2])
        last = jnp.where(upper, mine[3], got[3])
        halo = jnp.where(place == 0, last, first)
    else:
        halo = got[2]
    if stage + 1 < last_stage:
        send[0] = up
        send[1] = down
        send[2] = halo
    else:
        above, _, _ = place_of(last_stage)
        send[0] = jnp.where(above, down, up)
        send[1] = halo


def arrivals(stage, m, ykeep, got, held_in):
    before = [held_in[i] for i in range(4)]
    return receive(stage, ykeep[4], m, before, got[0], got[0], got[1], got[1])


def middle_kernel(stage, dev_z, bounds, got, held_in, ykeep, zkeep, *refs):
    pieces, sends, sums = refs[: len(bounds) - 1], refs[len(bounds) - 1 : -1], refs[-1]
    m = ykeep.shape[2]
    pos_z = lax.axis_index("gz")
    n = zkeep.shape[2]
    rows = arrivals(stage, m, ykeep, got, held_in)
    totals = []
    for kind in range(4):
        for piece, lo, hi in zip(pieces, bounds, bounds[1:]):
            sums[kind, lo:hi, :] = piece[:, kind, :]
        total = sums[kind]
        for i, row in enumerate(rows):
            if kind < 2:
                amount = jnp.sum(row * zkeep[5 + kind], axis=1, keepdims=True)
            else:
                amount = row[:, :1] if kind == 2 else row[:, n - 1 :]
            total = total + ykeep[i] * amount
        totals.append(total)
    up, down, head, tail = totals
    for by, send in enumerate(sends):
        ahead = pos_z + by + 1 < dev_z
        send[0] = jnp.where(ahead, up, down)
        send[1] = jnp.where(ahead, tail, head)


def held_kernel(stage, dev_z, rates_z, got, held_in, ykeep, zkeep, right_split, right):
    z = Line(down_sublanes(rates_z, right.shape[2]), lax.axis_index("gz"), dev_z, right.shape[2])
    z.vectors()
    for i, row in enumerate(along_lanes(z, arrivals(stage, ykeep.shape[2], ykeep, got, held_in))):
        right[:, i, :] = row
        right[:, 4 + i, :] = zkeep[i]
    b = right[...]
    hi = b.astype(BF16).astype(F32)
    lo = b - hi
    right_split[...] = jnp.concatenate([hi, hi, lo, lo], axis=1).astype(BF16)


def final_kernel(dev_z, bounds, right, ykeep, zkeep, *rest):
    gots, rest = rest[: dev_z - 1], rest[dev_z - 1 :]
    local, (out_hbm, out, out_sems, left) = rest[:-4], rest[-4:]
    planes, m, n = out.shape
    pos_z = lax.axis_index("gz")
    for i in range(4):
        left[:, i, :] = ykeep[i]
    reach = zkeep[4]
    up, down = jnp.zeros_like(gots[0][0]), jnp.zeros_like(gots[0][0])
    scale = jnp.ones_like(reach)
    for by in range(dev_z - 1):
        up = up + jnp.where(pos_z > by, scale * gots[by][0], 0.0)
        behind = gots[dev_z - 2 - by]
        down = down + jnp.where(pos_z + by + 1 < dev_z, scale * behind[0], 0.0)
        scale = scale * reach
    left[:, 4, :] = up
    left[:, 5, :] = down
    left[:, 6, :] = jnp.where(pos_z > 0, gots[0][1], 0.0)
    left[:, 7, :] = jnp.where(pos_z < dev_z - 1, gots[-1][1], 0.0)

    cuts = [planes * c // 16 for c in CUTS]
    stores = []
    for i, (lo, hi) in enumerate(zip(cuts, cuts[1:])):
        for k in range(lo, hi):
            a = left[k]
            a_hi = a.astype(BF16).astype(F32)
            a_lo = a - a_hi
            a = jnp.concatenate([a_hi, a_lo, a_hi, a_lo], axis=0).astype(BF16)
            piece = sum(k >= bound for bound in bounds[1:])
            out[k] = local[piece][k - bounds[piece]] + dot(a, right[k], 0, 0)
        some = pl.ds(lo, hi - lo)
        stores.append(pltpu.make_async_copy(out.at[some], out_hbm.at[some], out_sems.at[i]))
        stores[i].start()
    for store in stores:
        store.wait()


def per_device(x, rates_y, rates_z):
    planes, m, n = x.shape
    dev_y, dev_z = lax.axis_size("gy"), lax.axis_size("gz")
    whole = pl.BlockSpec(memory_space=pltpu.VMEM)

    def params():
        return pltpu.CompilerParams(vmem_limit_bytes=VMEM)

    def cost(flops, moved):
        return pl.CostEstimate(flops=flops, bytes_accessed=moved, transcendentals=0)

    def shape(*dims):
        return jax.ShapeDtypeStruct(dims, F32)

    cells = planes * m * n
    hbm = pl.BlockSpec(memory_space=pltpu.HBM)
    hbm = pl.BlockSpec(memory_space=pltpu.HBM)
    x = pl.pallas_call(
        fetch_kernel,
        in_specs=[hbm],
        out_specs=whole,
        out_shape=shape(planes, m, n),
        scratch_shapes=[pltpu.SemaphoreType.DMA((2,))],
        compiler_params=pltpu.CompilerParams(vmem_limit_bytes=FETCH_VMEM),
        cost_estimate=cost(4, 8 * cells),
        name="fetch",
    )(x)
    send = pl.pallas_call(
        functools.partial(moments_kernel, dev_y),
        in_specs=[whole, whole],
        out_specs=whole,
        out_shape=shape(4, planes, n),
        scratch_shapes=[
            pltpu.VMEM((planes, n), F32),
            pltpu.VMEM((planes, 8, n), F32),
            pltpu.VMEM((planes, 8, n), F32),
        ],
        compiler_params=params(),
        cost_estimate=cost(4 * cells, 4 * cells),
        name="moments",
    )(rates_y, x)
    stages = dev_y.bit_length() - 1
    bounds = [planes * i // stages for i in range(stages + 1)]
    parts, pieces = [], []
    held_in = None
    for stage in range(stages):
        lo, hi = bounds[stage], bounds[stage + 1]
        got = lax.ppermute(send, "gy", [(i, i ^ (1 << stage)) for i in range(dev_y)])
        first = stage == 0
        outs = [shape(hi - lo, m, n), shape(hi - lo, 8, m)]
        if first:
            given = (rates_y, rates_z, x)
            in_specs = [whole] * 3
            outs += [
                shape(5, planes, m),
                shape(7, planes, n),
                shape(7, planes, m),
                shape(8, planes, n),
                shape(planes, 8, n),
            ]
        else:
            given = (x, *tables, send)
            in_specs = [whole] * 5
        part, piece, *rest = pl.pallas_call(
            functools.partial(local_kernel, dev_y, dev_z, lo, hi),
            in_specs=in_specs,
            out_specs=[whole] * len(outs),
            out_shape=outs,
            scratch_shapes=[pltpu.VMEM((2, m, n), F32)],
            compiler_params=params(),
            cost_estimate=cost(12 * (hi - lo) * m * m * n, 8 * (hi - lo) * m * n),
            name="local",
        )(*given)
        parts.append(part)
        pieces.append(piece)
        if first:
            ykeep, zkeep, *tables = rest
        if stage + 1 < stages:
            send, held_in = pl.pallas_call(
                functools.partial(combine_kernel, stage, stages - 1, m),
                in_specs=[whole] * (4 if first else 5),
                out_specs=[whole] * 2,
                out_shape=[shape(3 if stage + 2 < stages else 2, planes, n), shape(4, planes, n)],
                compiler_params=params(),
                cost_estimate=cost(planes * n * 20, planes * n * 64),
                name="combine",
            )(send, got, *(() if first else (held_in,)), ykeep, piece)
    sends = pl.pallas_call(
        functools.partial(middle_kernel, stages - 1, dev_z, bounds),
        in_specs=[whole] * (4 + stages),
        out_specs=[whole] * (dev_z - 1),
        out_shape=[shape(2, planes, m)] * (dev_z - 1),
        scratch_shapes=[pltpu.VMEM((4, planes, m), F32)],
        compiler_params=params(),
        cost_estimate=cost(planes * n * 100, planes * n * 100),
        name="middle",
    )(got, held_in, ykeep, zkeep, *pieces)
    got_z = [
        lax.ppermute(send, "gz", [(i, (i + by + 1) % dev_z) for i in range(dev_z)])
        for by, send in enumerate(sends)
    ]
    held = pl.pallas_call(
        functools.partial(held_kernel, stages - 1, dev_z),
        in_specs=[whole] * 5,
        out_specs=whole,
        out_shape=jax.ShapeDtypeStruct((planes, 32, n), BF16),
        scratch_shapes=[pltpu.VMEM((planes, 8, n), F32)],
        compiler_params=params(),
        cost_estimate=cost(planes * n * 400, planes * n * 100),
        name="held",
    )(rates_z, got, held_in, ykeep, zkeep)
    return pl.pallas_call(
        functools.partial(final_kernel, dev_z, bounds),
        in_specs=[whole] * (dev_z + 2 + stages),
        out_specs=hbm,
        out_shape=shape(planes, m, n),
        scratch_shapes=[
            pltpu.VMEM((planes, m, n), F32),
            pltpu.SemaphoreType.DMA((len(CUTS) - 1,)),
            pltpu.VMEM((planes, 8, m), F32),
        ],
        compiler_params=params(),
        cost_estimate=cost(64 * cells, 8 * cells),
        name="final",
    )(held, ykeep, zkeep, *got_z, *parts)


def solution(mesh):
    return jax.shard_map(
        per_device,
        mesh=mesh,
        in_specs=(P(None, "gy", "gz"), P(), P()),
        out_specs=P(None, "gy", "gz"),
        check_vma=False,
    )
```
